32 devices in a mesh: node: 4 (over y, core), fsdp: 8 (over z, x).
Axes of the slice: x: 2, y: 2, z: 4, core: 2. Of those that a mesh axis runs over, the one named last changes fastest.
Arguments:
- activations: bfloat16 [32768, 2560], P(('node', 'fsdp'))
- grad_out: bfloat16 [32768, 2560], P(('node', 'fsdp'))
Outputs:
- combined: float32 [2560, 2560], P('fsdp', 'node')
All inputs are finite; a program needn't handle non-finite values.
Results may differ from the reference program's by a relative error of at most 0.0003.
Values may be sent and summed in bfloat16 or wider, within the bound.
A program may use at most 256 MiB of HBM per device.

```python
import math
import jax
import jax.numpy as jnp
from jax import lax

D = 2560
TOK_DEV = 1024
COLS = 2560
TOKENS = 32768
N_NODE = 4
N_FSDP = 8


def shared_mixing(key):
    return jax.random.truncated_normal(jax.random.fold_in(key, 101), -4.0, 4.0, (TOKENS,), jnp.float32)


def block_ramp(factor):
    block = jnp.arange(TOKENS) // TOK_DEV
    node_pos = (block // N_FSDP).astype(jnp.float32) / max(N_NODE - 1, 1)
    fsdp_pos = (block % N_FSDP).astype(jnp.float32) / max(N_FSDP - 1, 1)
    return jnp.exp(math.log(factor) * (node_pos + fsdp_pos))


def base_noise(key, count):
    return jax.random.truncated_normal(key, -4.0, 4.0, (TOKENS, count), jnp.float32)


def draw_activations(key, part):
    mixing = shared_mixing(key)
    key = jax.random.fold_in(key, 1)
    direction = jax.random.truncated_normal(jax.random.fold_in(key, 2), -4.0, 4.0, (D,), jnp.float32)
    feature_scale = jnp.exp(jax.random.uniform(jax.random.fold_in(key, 3), (D,), jnp.float32, math.log(0.3), math.log(3.0)))
    strength = float(TOK_DEV * N_FSDP) ** (-0.25)
    noise = base_noise(jax.random.fold_in(key, 4), D)
    values = noise + strength * mixing[:, None] * direction[None, :]
    return (values * feature_scale[None, :]).astype(jnp.bfloat16)


def draw_grad_out(key, part):
    mixing = shared_mixing(key)
    key = jax.random.fold_in(key, 2)
    direction = jax.random.truncated_normal(jax.random.fold_in(key, 5), -4.0, 4.0, (COLS,), jnp.float32)
    column_scale = jnp.exp(jax.random.uniform(jax.random.fold_in(key, 6), (COLS,), jnp.float32, math.log(0.3), math.log(3.0)))
    strength = float(TOK_DEV * N_FSDP) ** (-0.25)
    norm = 2.0 / math.sqrt(float(TOKENS))
    noise = base_noise(jax.random.fold_in(key, 7), COLS)
    ramp = block_ramp(3.0)
    values = noise + strength * mixing[:, None] * direction[None, :]
    return (values * column_scale[None, :] * (ramp * norm)[:, None]).astype(jnp.bfloat16)


def setup_inputs(seed: int = 0) -> dict:
    streams_of = jax.random.split(jax.random.key(seed), 3)
    activations = draw_activations(jax.random.fold_in(streams_of[2], 71), 0)
    grad_out = draw_grad_out(jax.random.fold_in(streams_of[2], 71), 0)
    return dict(activations=activations, grad_out=grad_out)


def node_gradient(x_node, dy_node):
    x_blocks = x_node.reshape(N_FSDP, TOK_DEV, D)
    dy_blocks = dy_node.reshape(N_FSDP, TOK_DEV, COLS)

    def accumulate(total, pair):
        product = lax.dot_general(pair[0], pair[1], (((0,), (0,)), ((), ())), preferred_element_type=jnp.float32)
        return total + product, None

    start = jnp.zeros((D, COLS), jnp.float32)
    total, _ = lax.scan(accumulate, start, (x_blocks, dy_blocks))
    return total


def reference(activations, grad_out):
    x_nodes = activations.reshape(N_NODE, N_FSDP * TOK_DEV, D)
    dy_nodes = grad_out.reshape(N_NODE, N_FSDP * TOK_DEV, COLS)
    vectors = lax.map(lambda pair: node_gradient(pair[0], pair[1]), (x_nodes, dy_nodes))
    levels = int(N_NODE).bit_length() - 1
    for level in range(levels):
        half = vectors.shape[0] // 2
        first = vectors[:half]
        second = vectors[half:]
        inner = jnp.sum(first * second, axis=(1, 2))
        first_sq = jnp.sum(first * first, axis=(1, 2))
        second_sq = jnp.sum(second * second, axis=(1, 2))
        coef_first = 1.0 - inner / (2.0 * (first_sq + 1e-6))
        coef_second = 1.0 - inner / (2.0 * (second_sq + 1e-6))
        vectors = coef_first[:, None, None] * first + coef_second[:, None, None] * second
    return vectors[0]
```

```python
import functools

import jax
import jax.numpy as jnp
from jax import lax
from jax.experimental import pallas as pl
from jax.experimental.pallas import tpu as pltpu
from jax.sharding import PartitionSpec as P

EPS = 1e-06
MESH = pl.DeviceIdType.MESH
TOP = 2.0**14
Z_SIZE = 4


def ring_place(position, count):
    x_size = count // Z_SIZE
    inner = x_size - 1
    past = (position + count - Z_SIZE) // count
    rest = (position - Z_SIZE + count) % count
    line = rest // inner
    step = rest % inner
    odd = line % 2
    x = (1 - odd) * (1 + step) + odd * (x_size - 1 - step)
    z = Z_SIZE - 1 - line
    return past * (z * x_size + x) + (1 - past) * position * x_size


def ring_position(index, count):
    x_size = count // Z_SIZE
    inner = x_size - 1
    z = index // x_size
    x = index % x_size
    past = (x + inner) // x_size
    line = Z_SIZE - 1 - z
    odd = line % 2
    step = (1 - odd) * (x - 1) + odd * (x_size - 1 - x)
    return past * (Z_SIZE + line * inner + step) + (1 - past) * z


def encode(value, top):
    x = value * (TOP / top)
    square = x * x
    fourth = square * square
    eighth = fourth * fourth
    return jnp.where(x < 0, -eighth, eighth).astype(jnp.bfloat16)


def decode(code, top):
    y = code.astype(jnp.float32)
    root = lax.rsqrt(lax.rsqrt(jnp.maximum(jnp.abs(y), 1e-37)))
    value = root * lax.rsqrt(root) * (top * (1.0 / TOP))
    return jnp.where(y < 0, -value, value)


def kernel(
    nodes, count, at_ref, g_ref, out_ref,
    sent, came, sent_top, came_top, acc, own, gathered, sums_mine, sums_came,
    send_sem, recv_sem, top_send, top_recv, swap_send, swap_recv, sum_send, sum_recv,
):
    node = lax.axis_index("node")
    place = lax.axis_index("fsdp")
    rows, cols = acc.shape
    me = ring_position(place, count)
    right = ring_place((me + 1) % count, count)
    left = ring_place((me + count - 1) % count, count)
    half = count // 2

    barrier = pltpu.get_barrier_semaphore()
    for k in range(1, count):
        pl.semaphore_signal(barrier, inc=1, device_id=(node, (place + k) % count), device_id_type=MESH)
    for k in range(1, nodes):
        pl.semaphore_signal(barrier, inc=1, device_id=((node + k) % nodes, place), device_id_type=MESH)
    pl.semaphore_wait(barrier, count + nodes - 2)

    def product(owner, block):
        if g_ref.ndim == 3:
            g = g_ref[block]
        else:
            g = g_ref[:, pl.ds(pl.multiple_of(block * cols, cols), cols)]
        acc[...] = jnp.dot(at_ref[owner], g, preferred_element_type=jnp.float32)

    def copies(side, block, step):
        target = (node, right if side == 0 else left)
        data = pltpu.make_async_remote_copy(
            src_ref=sent.at[side, block, step], dst_ref=came.at[side, block, step],
            send_sem=send_sem.at[side, block, step], recv_sem=recv_sem.at[side, block, step],
            device_id=target, device_id_type=MESH)
        top = pltpu.make_async_remote_copy(
            src_ref=sent_top.at[side, block, step], dst_ref=came_top.at[side, block, step],
            send_sem=top_send.at[side, block, step], recv_sem=top_recv.at[side, block, step],
            device_id=target, device_id_type=MESH)
        return data, top

    def add_arrived(side, block, step):
        data, top = copies(side, block, step)
        top.wait_recv()
        data.wait_recv()
        largest = came_top[side, block, step][0:1, 0:1].astype(jnp.float32)
        acc[...] += decode(came[side, block, step], largest)

    def hops(side, parity):
        return half if side == parity else count - 1 - half

    def send_on(side, parity, block, step):
        distance = hops(side, parity) - step
        far = (me + distance) % count if side == 0 else (me + count - distance) % count
        product(ring_place(far, count), block)

        @pl.when(step > 0)
        def _():
            add_arrived(side, block, step - 1)

        largest = jnp.maximum(jnp.max(jnp.abs(acc[...]), axis=(0, 1), keepdims=True), 1e-30)
        tile = jnp.broadcast_to(largest, (16, 128)).astype(jnp.bfloat16)
        sent_top[side, block, step] = tile
        sent[side, block, step] = encode(acc[...], tile[0:1, 0:1].astype(jnp.float32))
        data, top = copies(side, block, step)
        top.start()
        data.start()

    def swap(block):
        return pltpu.make_async_remote_copy(
            src_ref=own.at[block], dst_ref=gathered.at[node],
            send_sem=swap_send.at[block], recv_sem=swap_recv.at[node],
            device_id=(block, place), device_id_type=MESH)

    def finish(parity, block):
        product(place, block)
        for side in range(2):
            add_arrived(side, block, hops(side, parity) - 1)

        @pl.when(block != node)
        def _():
            own[block] = acc[...]
            swap(block).start()

        @pl.when(block == node)
        def _():
            gathered[block] = acc[...]

    @pl.loop(0, nodes // 2)
    def _(pair):
        @pl.loop(0, half)
        def _(step):
            for parity in range(2):
                for side in range(2):
                    if side == parity:
                        send_on(side, parity, 2 * pair + parity, step)
                    else:
                        pl.when(step < half - 1)(
                            functools.partial(send_on, side, parity, 2 * pair + parity, step))

            @pl.when((step == 0) & (pair > 0))
            def _():
                for parity in range(2):
                    finish(parity, 2 * pair - 2 + parity)

    for parity in range(2):
        finish(parity, nodes - 2 + parity)

    @pl.loop(1, nodes)
    def _(k):
        other = (node + k) % nodes
        pltpu.make_async_remote_copy(
            src_ref=own.at[other], dst_ref=gathered.at[other],
            send_sem=swap_send.at[other], recv_sem=swap_recv.at[other],
            device_id=(other, place), device_id_type=MESH).wait_recv()

    def exchange(level, stage, size):
        def copy(k):
            far = (node, (place + k) % count) if stage == 0 else ((node + k) % nodes, place)
            return pltpu.make_async_remote_copy(
                src_ref=sums_mine.at[level, stage], dst_ref=sums_came.at[level, stage, k],
                send_sem=sum_send.at[level, stage, k], recv_sem=sum_recv.at[level, stage, k],
                device_id=far, device_id_type=MESH)

        for k in range(1, size):
            copy(k).start()
        total = sums_mine[level, stage]
        for k in range(1, size):
            copy(k).wait_recv()
            total = total + sums_came[level, stage, k]
        for k in range(1, size):
            copy(k).wait_send()
        return total

    def whole_sum(value):
        return jnp.sum(jnp.sum(value, axis=0, keepdims=True), axis=1, keepdims=True)

    levels = nodes.bit_length() - 1
    left_over = nodes
    for level in range(levels):
        left_over //= 2
        tile = jnp.zeros(sums_mine.shape[2:], jnp.float32)
        line = lax.broadcasted_iota(jnp.int32, tile.shape, 0)
        for j in range(left_over):
            first = gathered[j]
            second = gathered[j + left_over]
            for i, term in enumerate((first * second, first * first, second * second)):
                tile = jnp.where(line == 3 * j + i, whole_sum(term), tile)
        sums_mine[level, 0] = tile
        sums_mine[level, 1] = exchange(level, 0, count)
        total = exchange(level, 1, nodes)
        for j in range(left_over):
            inner = total[3 * j : 3 * j + 1, 0:1]
            first_sq = total[3 * j + 1 : 3 * j + 2, 0:1]
            second_sq = total[3 * j + 2 : 3 * j + 3, 0:1]
            coef_first = 1.0 - inner / (2.0 * (first_sq + EPS))
            coef_second = 1.0 - inner / (2.0 * (second_sq + EPS))
            mixed = coef_first * gathered[j] + coef_second * gathered[j + left_over]
            if left_over == 1:
                out_ref[...] = mixed
            else:
                gathered[j] = mixed

    @pl.loop(1, nodes)
    def _(k):
        swap((node + k) % nodes).wait_send()

    @pl.loop(0, nodes // 2)
    def _(pair):
        for parity in range(2):
            for side in range(2):
                @pl.loop(0, hops(side, parity))
                def _(step):
                    data, top = copies(side, 2 * pair + parity, step)
                    top.wait_send()
                    data.wait_send()


def solution(mesh):
    nodes, count = mesh.shape["node"], mesh.shape["fsdp"]

    def local(activations, grad_out):
        tokens, features = activations.shape
        columns = grad_out.shape[1]
        rows, cols = features // count, columns // nodes
        half = count // 2
        levels = nodes.bit_length() - 1
        turned = activations.T.reshape(count, rows, tokens)
        if cols % 128:
            grad_out = grad_out.reshape(tokens, nodes, cols).transpose(1, 0, 2)
        lines = -(-3 * nodes // 2 // 8) * 8
        hop = (2, nodes, half)
        dma = pltpu.SemaphoreType.DMA
        return pl.pallas_call(
            functools.partial(kernel, nodes, count),
            out_shape=jax.ShapeDtypeStruct((rows, cols), jnp.float32),
            in_specs=[pl.BlockSpec(memory_space=pltpu.VMEM)] * 2,
            out_specs=pl.BlockSpec(memory_space=pltpu.VMEM),
            scratch_shapes=[
                pltpu.VMEM(hop + (rows, cols), jnp.bfloat16),
                pltpu.VMEM(hop + (rows, cols), jnp.bfloat16),
                pltpu.VMEM(hop + (16, 128), jnp.bfloat16),
                pltpu.VMEM(hop + (16, 128), jnp.bfloat16),
                pltpu.VMEM((rows, cols), jnp.float32),
                pltpu.VMEM((nodes, rows, cols), jnp.float32),
                pltpu.VMEM((nodes, rows, cols), jnp.float32),
                pltpu.VMEM((levels, 2, lines, 128), jnp.float32),
                pltpu.VMEM((levels, 2, max(nodes, count), lines, 128), jnp.float32),
                dma(hop), dma(hop), dma(hop), dma(hop),
                dma((nodes,)), dma((nodes,)),
                dma((levels, 2, max(nodes, count))), dma((levels, 2, max(nodes, count))),
            ],
            compiler_params=pltpu.CompilerParams(
                collective_id=0, has_side_effects=True, vmem_limit_bytes=60 * 2**20),
        )(turned, grad_out)

    in_specs = (P(("node", "fsdp"), None), P(("node", "fsdp"), None))
    return jax.shard_map(local, mesh=mesh, in_specs=in_specs, out_specs=P("fsdp", "node"), check_vma=False)
```

```python
import functools

import jax
import jax.numpy as jnp
from jax import lax
from jax.experimental import pallas as pl
from jax.experimental.pallas import tpu as pltpu
from jax.sharding import PartitionSpec as P

EPS = 1e-06
MESH = pl.DeviceIdType.MESH
TOP = 2.0**14
Z_SIZE = 4
CHUNK = 16


def ring_place(position, count):
    x_size = count // Z_SIZE
    inner = x_size - 1
    past = (position + count - Z_SIZE) // count
    rest = (position - Z_SIZE + count) % count
    line = rest // inner
    step = rest % inner
    odd = line % 2
    x = (1 - odd) * (1 + step) + odd * (x_size - 1 - step)
    z = Z_SIZE - 1 - line
    return past * (z * x_size + x) + (1 - past) * position * x_size


def ring_position(index, count):
    x_size = count // Z_SIZE
    inner = x_size - 1
    z = index // x_size
    x = index % x_size
    past = (x + inner) // x_size
    line = Z_SIZE - 1 - z
    odd = line % 2
    step = (1 - odd) * (x - 1) + odd * (x_size - 1 - x)
    return past * (Z_SIZE + line * inner + step) + (1 - past) * z


def encode(value, scale):
    x = value * scale
    square = x * x
    fourth = square * square
    eighth = fourth * fourth
    return jnp.where(x < 0, -eighth, eighth).astype(jnp.bfloat16)


def decode(code, top):
    y = code.astype(jnp.float32)
    root = lax.rsqrt(lax.rsqrt(jnp.maximum(jnp.abs(y), 1e-37)))
    value = root * lax.rsqrt(root) * (top * (1.0 / TOP))
    return jnp.where(y < 0, -value, value)


def kernel(
    nodes, count, at_ref, g_ref, out_ref,
    sent, came, sent_top, came_top, acc, peaks, own, gathered, sums_mine, sums_came,
    send_sem, recv_sem, top_send, top_recv, swap_send, swap_recv, sum_send, sum_recv,
):
    node = lax.axis_index("node")
    place = lax.axis_index("fsdp")
    rows, cols = acc.shape
    me = ring_position(place, count)
    right = ring_place((me + 1) % count, count)
    left = ring_place((me + count - 1) % count, count)
    half = count // 2

    barrier = pltpu.get_barrier_semaphore()
    for k in range(1, count):
        pl.semaphore_signal(barrier, inc=1, device_id=(node, (place + k) % count), device_id_type=MESH)
    for k in range(1, nodes):
        pl.semaphore_signal(barrier, inc=1, device_id=((node + k) % nodes, place), device_id_type=MESH)
    pl.semaphore_wait(barrier, count + nodes - 2)

    def product(owner, block):
        if g_ref.ndim == 3:
            g = g_ref[block]
        else:
            g = g_ref[:, pl.ds(pl.multiple_of(block * cols, cols), cols)]
        acc[...] = jnp.dot(at_ref[owner], g, preferred_element_type=jnp.float32)

    def copies(side, block, step):
        target = (node, right if side == 0 else left)
        data = pltpu.make_async_remote_copy(
            src_ref=sent.at[side, block, step], dst_ref=came.at[side, block, step],
            send_sem=send_sem.at[side, block, step], recv_sem=recv_sem.at[side, block, step],
            device_id=target, device_id_type=MESH)
        top = pltpu.make_async_remote_copy(
            src_ref=sent_top.at[side, block, step], dst_ref=came_top.at[side, block, step],
            send_sem=top_send.at[side, block, step], recv_sem=top_recv.at[side, block, step],
            device_id=target, device_id_type=MESH)
        return data, top

    def by_chunk(body, start=None):
        def step(i, carry):
            return body(pl.ds(pl.multiple_of(i * CHUNK, CHUNK), CHUNK), carry)

        return lax.fori_loop(0, rows // CHUNK, step, start, unroll=2)

    def arrived(side, block, step):
        data, top = copies(side, block, step)
        top.wait_recv()
        data.wait_recv()
        return came_top[side, block, step][0:1, 0:1].astype(jnp.float32)

    def hops(side, parity):
        return half if side == parity else count - 1 - half

    def send_on(side, parity, block, step):
        distance = hops(side, parity) - step
        far = (me + distance) % count if side == 0 else (me + count - distance) % count
        product(ring_place(far, count), block)

        @pl.when(step > 0)
        def _():
            top = arrived(side, block, step - 1)

            def add(part, peak):
                value = acc[part, :] + decode(came[side, block, step - 1, part, :], top)
                acc[part, :] = value
                return jnp.maximum(peak, jnp.abs(value))

            peaks[...] = by_chunk(add, jnp.zeros(peaks.shape, jnp.float32))

        @pl.when(step == 0)
        def _():
            peaks[...] = by_chunk(
                lambda part, peak: jnp.maximum(peak, jnp.abs(acc[part, :])), jnp.zeros(peaks.shape, jnp.float32))

        largest = jnp.maximum(jnp.max(peaks[...], axis=(0, 1), keepdims=True), 1e-30)
        tile = jnp.broadcast_to(largest, (16, 128)).astype(jnp.bfloat16)
        sent_top[side, block, step] = tile
        scale = TOP / tile[0:1, 0:1].astype(jnp.float32)

        def code(part, carry):
            sent[side, block, step, part, :] = encode(acc[part, :], scale)

        by_chunk(code)
        data, top = copies(side, block, step)
        top.start()
        data.start()

    def swap(block):
        return pltpu.make_async_remote_copy(
            src_ref=own.at[block], dst_ref=gathered.at[node],
            send_sem=swap_send.at[block], recv_sem=swap_recv.at[node],
            device_id=(block, place), device_id_type=MESH)

    def finish(parity, block):
        product(place, block)
        steps = [hops(side, parity) - 1 for side in range(2)]
        tops = [arrived(side, block, steps[side]) for side in range(2)]

        def total(part):
            value = acc[part, :]
            for side in range(2):
                value = value + decode(came[side, block, steps[side], part, :], tops[side])
            return value

        @pl.when(block != node)
        def _():
            def store(part, carry):
                own[block, part, :] = total(part)

            by_chunk(store)
            swap(block).start()

        @pl.when(block == node)
        def _():
            def store(part, carry):
                gathered[block, part, :] = total(part)

            by_chunk(store)

    def pair_at(turn):
        return (node // 2 + 1 + turn) % (nodes // 2)

    @pl.loop(0, nodes // 2)
    def _(turn):
        pair = pair_at(turn)

        @pl.loop(0, half)
        def _(step):
            for parity in range(2):
                for side in range(2):
                    if side == parity:
                        send_on(side, parity, 2 * pair + parity, step)
                    else:
                        pl.when(step < half - 1)(
                            functools.partial(send_on, side, parity, 2 * pair + parity, step))

            @pl.when((step == 0) & (turn > 0))
            def _():
                for parity in range(2):
                    finish(parity, 2 * pair_at(turn - 1) + parity)

    for parity in range(2):
        finish(parity, 2 * pair_at(nodes // 2 - 1) + parity)

    @pl.loop(1, nodes)
    def _(k):
        other = (node + k) % nodes
        pltpu.make_async_remote_copy(
            src_ref=own.at[other], dst_ref=gathered.at[other],
            send_sem=swap_send.at[other], recv_sem=swap_recv.at[other],
            device_id=(other, place), device_id_type=MESH).wait_recv()

    def exchange(level, stage, size):
        def copy(k):
            far = (node, (place + k) % count) if stage == 0 else ((node + k) % nodes, place)
            return pltpu.make_async_remote_copy(
                src_ref=sums_mine.at[level, stage], dst_ref=sums_came.at[level, stage, k],
                send_sem=sum_send.at[level, stage, k], recv_sem=sum_recv.at[level, stage, k],
                device_id=far, device_id_type=MESH)

        for k in range(1, size):
            copy(k).start()
        total = sums_mine[level, stage]
        for k in range(1, size):
            copy(k).wait_recv()
            total = total + sums_came[level, stage, k]
        for k in range(1, size):
            copy(k).wait_send()
        return total

    def whole_sum(value):
        return jnp.sum(jnp.sum(value, axis=0, keepdims=True), axis=1, keepdims=True)

    levels = nodes.bit_length() - 1
    left_over = nodes
    for level in range(levels):
        left_over //= 2
        tile = jnp.zeros(sums_mine.shape[2:], jnp.float32)
        line = lax.broadcasted_iota(jnp.int32, tile.shape, 0)
        for j in range(left_over):
            def add(part, sums):
                first = gathered[j, part, :]
                second = gathered[j + left_over, part, :]
                return sums[0] + first * second, sums[1] + first * first, sums[2] + second * second

            for i, term in enumerate(by_chunk(add, (jnp.zeros(peaks.shape, jnp.float32),) * 3)):
                tile = jnp.where(line == 3 * j + i, whole_sum(term), tile)
        sums_mine[level, 0] = tile
        sums_mine[level, 1] = exchange(level, 0, count)
        total = exchange(level, 1, nodes)
        for j in range(left_over):
            inner = total[3 * j : 3 * j + 1, 0:1]
            first_sq = total[3 * j + 1 : 3 * j + 2, 0:1]
            second_sq = total[3 * j + 2 : 3 * j + 3, 0:1]
            coef_first = 1.0 - inner / (2.0 * (first_sq + EPS))
            coef_second = 1.0 - inner / (2.0 * (second_sq + EPS))

            def mix(part, carry):
                mixed = coef_first * gathered[j, part, :] + coef_second * gathered[j + left_over, part, :]
                if left_over == 1:
                    out_ref[part, :] = mixed
                else:
                    gathered[j, part, :] = mixed

            by_chunk(mix)

    @pl.loop(1, nodes)
    def _(k):
        swap((node + k) % nodes).wait_send()

    @pl.loop(0, nodes // 2)
    def _(pair):
        for parity in range(2):
            for side in range(2):
                @pl.loop(0, hops(side, parity))
                def _(step):
                    data, top = copies(side, 2 * pair + parity, step)
                    top.wait_send()
                    data.wait_send()


def solution(mesh):
    nodes, count = mesh.shape["node"], mesh.shape["fsdp"]

    def local(activations, grad_out):
        tokens, features = activations.shape
        columns = grad_out.shape[1]
        rows, cols = features // count, columns // nodes
        half = count // 2
        levels = nodes.bit_length() - 1
        turned = activations.T.reshape(count, rows, tokens)
        if cols % 128:
            grad_out = grad_out.reshape(tokens, nodes, cols).transpose(1, 0, 2)
        lines = -(-3 * nodes // 2 // 8) * 8
        hop = (2, nodes, half)
        dma = pltpu.SemaphoreType.DMA
        return pl.pallas_call(
            functools.partial(kernel, nodes, count),
            out_shape=jax.ShapeDtypeStruct((rows, cols), jnp.float32),
            in_specs=[pl.BlockSpec(memory_space=pltpu.VMEM)] * 2,
            out_specs=pl.BlockSpec(memory_space=pltpu.VMEM),
            scratch_shapes=[
                pltpu.VMEM(hop + (rows, cols), jnp.bfloat16),
                pltpu.VMEM(hop + (rows, cols), jnp.bfloat16),
                pltpu.VMEM(hop + (16, 128), jnp.bfloat16),
                pltpu.VMEM(hop + (16, 128), jnp.bfloat16),
                pltpu.VMEM((rows, cols), jnp.float32),
                pltpu.VMEM((CHUNK, cols), jnp.float32),
                pltpu.VMEM((nodes, rows, cols), jnp.float32),
                pltpu.VMEM((nodes, rows, cols), jnp.float32),
                pltpu.VMEM((levels, 2, lines, 128), jnp.float32),
                pltpu.VMEM((levels, 2, max(nodes, count), lines, 128), jnp.float32),
                dma(hop), dma(hop), dma(hop), dma(hop),
                dma((nodes,)), dma((nodes,)),
                dma((levels, 2, max(nodes, count))), dma((levels, 2, max(nodes, count))),
            ],
            compiler_params=pltpu.CompilerParams(
                collective_id=0, has_side_effects=True, vmem_limit_bytes=60 * 2**20),
        )(turned, grad_out)

    in_specs = (P(("node", "fsdp"), None), P(("node", "fsdp"), None))
    return jax.shard_map(local, mesh=mesh, in_specs=in_specs, out_specs=P("fsdp", "node"), check_vma=False)
```

```python
import functools

import jax
import jax.numpy as jnp
from jax import lax
from jax.experimental import pallas as pl
from jax.experimental.pallas import tpu as pltpu
from jax.sharding import PartitionSpec as P

EPS = 1e-06
MESH = pl.DeviceIdType.MESH
TOP = 2.0**14
Z_SIZE = 4
CHUNK = 16


def ring_place(position, count):
    x_size = count // Z_SIZE
    inner = x_size - 1
    past = (position + count - Z_SIZE) // count
    rest = (position - Z_SIZE + count) % count
    line = rest // inner
    step = rest % inner
    odd = line % 2
    x = (1 - odd) * (1 + step) + odd * (x_size - 1 - step)
    z = Z_SIZE - 1 - line
    return past * (z * x_size + x) + (1 - past) * position * x_size


def ring_position(index, count):
    x_size = count // Z_SIZE
    inner = x_size - 1
    z = index // x_size
    x = index % x_size
    past = (x + inner) // x_size
    line = Z_SIZE - 1 - z
    odd = line % 2
    step = (1 - odd) * (x - 1) + odd * (x_size - 1 - x)
    return past * (Z_SIZE + line * inner + step) + (1 - past) * z


def encode(value, scale):
    x = value * scale
    square = x * x
    fourth = square * square
    eighth = fourth * fourth
    return jnp.where(x < 0, -eighth, eighth).astype(jnp.bfloat16)


def decode(code, top):
    y = code.astype(jnp.float32)
    root = lax.rsqrt(lax.rsqrt(jnp.maximum(jnp.abs(y), 1e-37)))
    value = root * lax.rsqrt(root) * (top * (1.0 / TOP))
    return jnp.where(y < 0, -value, value)


def kernel(
    nodes, count, a_ref, g_hbm, out_ref,
    raw, at_ref, g_ref, sent, came, sent_top, came_top, acc, peaks, own, gathered, sums_mine, sums_came,
    a_sem, g_sem, send_sem, recv_sem, top_send, top_recv, swap_send, swap_recv, sum_send, sum_recv,
):
    node = lax.axis_index("node")
    place = lax.axis_index("fsdp")
    rows, cols = acc.shape
    me = ring_position(place, count)
    right = ring_place((me + 1) % count, count)
    left = ring_place((me + count - 1) % count, count)
    half = count // 2

    x_size = count // Z_SIZE
    width = raw.shape[1] // Z_SIZE
    far_group = ring_place((me + half) % count, count) // x_size

    def pair_at(turn):
        return (node // 2 + 1 + turn) % (nodes // 2)

    def g_view(ref, block):
        if ref.ndim == 3:
            return ref.at[block]
        return ref.at[:, pl.ds(pl.multiple_of(block * cols, cols), cols)]

    def a_load(group):
        part = pl.ds(pl.multiple_of(group * width, 128), width)
        return pltpu.make_async_copy(a_ref.at[:, part], raw.at[:, part], a_sem.at[group])

    def g_load(block):
        return pltpu.make_async_copy(g_view(g_hbm, block), g_view(g_ref, block), g_sem.at[block])

    barrier = pltpu.get_barrier_semaphore()
    for k in range(1, count):
        pl.semaphore_signal(barrier, inc=1, device_id=(node, (place + k) % count), device_id_type=MESH)
    for k in range(1, nodes):
        pl.semaphore_signal(barrier, inc=1, device_id=((node + k) % nodes, place), device_id_type=MESH)
    a_load(far_group).start()
    for parity in range(2):
        g_load(2 * pair_at(0) + parity).start()
    for k in range(1, Z_SIZE):
        a_load((far_group + k) % Z_SIZE).start()

    @pl.loop(1, nodes // 2)
    def _(turn):
        for parity in range(2):
            g_load(2 * pair_at(turn) + parity).start()

    def transpose_group(group):
        a_load(group).wait()

        @pl.loop(0, width // 128)
        def _(i):
            part = pl.ds(pl.multiple_of(group * width + i * 128, 128), 128)
            at_ref[part, :] = raw[:, part].T

    transpose_group(far_group)
    pl.semaphore_wait(barrier, count + nodes - 2)

    def product(owner, block):
        mine = at_ref[pl.ds(pl.multiple_of(owner * rows, 16), rows), :]
        acc[...] = jnp.dot(mine, g_view(g_ref, block)[...], preferred_element_type=jnp.float32)

    def copies(side, block, step):
        target = (node, right if side == 0 else left)
        data = pltpu.make_async_remote_copy(
            src_ref=sent.at[side, block, step], dst_ref=came.at[side, block, step],
            send_sem=send_sem.at[side, block, step], recv_sem=recv_sem.at[side, block, step],
            device_id=target, device_id_type=MESH)
        top = pltpu.make_async_remote_copy(
            src_ref=sent_top.at[side, block, step], dst_ref=came_top.at[side, block, step],
            send_sem=top_send.at[side, block, step], recv_sem=top_recv.at[side, block, step],
            device_id=target, device_id_type=MESH)
        return data, top

    def by_chunk(body, start=None):
        def step(i, carry):
            return body(pl.ds(pl.multiple_of(i * CHUNK, CHUNK), CHUNK), carry)

        return lax.fori_loop(0, rows // CHUNK, step, start, unroll=2)

    def arrived(side, block, step):
        data, top = copies(side, block, step)
        top.wait_recv()
        data.wait_recv()
        return came_top[side, block, step][0:1, 0:1].astype(jnp.float32)

    def hops(side, parity):
        return half if side == parity else count - 1 - half

    def send_on(side, parity, block, step):
        distance = hops(side, parity) - step
        far = (me + distance) % count if side == 0 else (me + count - distance) % count
        product(ring_place(far, count), block)

        @pl.when(step > 0)
        def _():
            top = arrived(side, block, step - 1)

            def add(part, peak):
                value = acc[part, :] + decode(came[side, block, step - 1, part, :], top)
                acc[part, :] = value
                return jnp.maximum(peak, jnp.abs(value))

            peaks[...] = by_chunk(add, jnp.zeros(peaks.shape, jnp.float32))

        @pl.when(step == 0)
        def _():
            peaks[...] = by_chunk(
                lambda part, peak: jnp.maximum(peak, jnp.abs(acc[part, :])), jnp.zeros(peaks.shape, jnp.float32))

        largest = jnp.maximum(jnp.max(peaks[...], axis=(0, 1), keepdims=True), 1e-30)
        tile = jnp.broadcast_to(largest, (16, 128)).astype(jnp.bfloat16)
        sent_top[side, block, step] = tile
        scale = TOP / tile[0:1, 0:1].astype(jnp.float32)

        def code(part, carry):
            sent[side, block, step, part, :] = encode(acc[part, :], scale)

        by_chunk(code)
        data, top = copies(side, block, step)
        top.start()
        data.start()

    def swap(block):
        return pltpu.make_async_remote_copy(
            src_ref=own.at[block], dst_ref=gathered.at[node],
            send_sem=swap_send.at[block], recv_sem=swap_recv.at[node],
            device_id=(block, place), device_id_type=MESH)

    def prepare(parity, block):
        product(place, block)
        top = arrived(1 - parity, block, half - 2)

        def add(part, carry):
            own[block, part, :] = acc[part, :] + decode(came[1 - parity, block, half - 2, part, :], top)

        by_chunk(add)

    def finish(parity, block):
        top = arrived(parity, block, half - 1)

        def total(part):
            return own[block, part, :] + decode(came[parity, block, half - 1, part, :], top)

        @pl.when(block != node)
        def _():
            def store(part, carry):
                own[block, part, :] = total(part)

            by_chunk(store)
            swap(block).start()

        @pl.when(block == node)
        def _():
            def store(part, carry):
                gathered[block, part, :] = total(part)

            by_chunk(store)

    def finish_pair(turn):
        for parity in range(2):
            prepare(parity, 2 * pair_at(turn) + parity)
        for parity in range(2):
            finish(parity, 2 * pair_at(turn) + parity)

    @pl.loop(0, nodes // 2)
    def _(turn):
        pair = pair_at(turn)
        for parity in range(2):
            g_load(2 * pair + parity).wait()

        @pl.loop(0, half)
        def _(step):
            for side in range(2):
                send_on(side, side, 2 * pair + side, step)

            @pl.when((turn == 0) & (step == 0))
            def _():
                for k in range(1, Z_SIZE):
                    transpose_group((far_group + k) % Z_SIZE)

            @pl.when(step < half - 1)
            def _():
                for side in range(2):
                    send_on(side, 1 - side, 2 * pair + 1 - side, step)

            @pl.when((step == 0) & (turn > 0))
            def _():
                finish_pair(turn - 1)

    finish_pair(nodes // 2 - 1)

    @pl.loop(1, nodes)
    def _(k):
        other = (node + k) % nodes
        pltpu.make_async_remote_copy(
            src_ref=own.at[other], dst_ref=gathered.at[other],
            send_sem=swap_send.at[other], recv_sem=swap_recv.at[other],
            device_id=(other, place), device_id_type=MESH).wait_recv()

    def exchange(level, stage, size):
        def copy(k):
            far = (node, (place + k) % count) if stage == 0 else ((node + k) % nodes, place)
            return pltpu.make_async_remote_copy(
                src_ref=sums_mine.at[level, stage], dst_ref=sums_came.at[level, stage, k],
                send_sem=sum_send.at[level, stage, k], recv_sem=sum_recv.at[level, stage, k],
                device_id=far, device_id_type=MESH)

        for k in range(1, size):
            copy(k).start()
        total = sums_mine[level, stage]
        for k in range(1, size):
            copy(k).wait_recv()
            total = total + sums_came[level, stage, k]
        for k in range(1, size):
            copy(k).wait_send()
        return total

    def whole_sum(value):
        return jnp.sum(jnp.sum(value, axis=0, keepdims=True), axis=1, keepdims=True)

    levels = nodes.bit_length() - 1
    left_over = nodes
    for level in range(levels):
        left_over //= 2
        tile = jnp.zeros(sums_mine.shape[2:], jnp.float32)
        line = lax.broadcasted_iota(jnp.int32, tile.shape, 0)
        for j in range(left_over):
            def add(part, sums):
                first = gathered[j, part, :]
                second = gathered[j + left_over, part, :]
                return sums[0] + first * second, sums[1] + first * first, sums[2] + second * second

            for i, term in enumerate(by_chunk(add, (jnp.zeros(peaks.shape, jnp.float32),) * 3)):
                tile = jnp.where(line == 3 * j + i, whole_sum(term), tile)
        sums_mine[level, 0] = tile
        sums_mine[level, 1] = exchange(level, 0, count)
        total = exchange(level, 1, nodes)
        for j in range(left_over):
            inner = total[3 * j : 3 * j + 1, 0:1]
            first_sq = total[3 * j + 1 : 3 * j + 2, 0:1]
            second_sq = total[3 * j + 2 : 3 * j + 3, 0:1]
            coef_first = 1.0 - inner / (2.0 * (first_sq + EPS))
            coef_second = 1.0 - inner / (2.0 * (second_sq + EPS))

            def mix(part, carry):
                mixed = coef_first * gathered[j, part, :] + coef_second * gathered[j + left_over, part, :]
                if left_over == 1:
                    out_ref[part, :] = mixed
                else:
                    gathered[j, part, :] = mixed

            by_chunk(mix)

    @pl.loop(1, nodes)
    def _(k):
        swap((node + k) % nodes).wait_send()

    @pl.loop(0, nodes // 2)
    def _(pair):
        for parity in range(2):
            for side in range(2):
                @pl.loop(0, hops(side, parity))
                def _(step):
                    data, top = copies(side, 2 * pair + parity, step)
                    top.wait_send()
                    data.wait_send()


def solution(mesh):
    nodes, count = mesh.shape["node"], mesh.shape["fsdp"]

    def local(activations, grad_out):
        tokens, features = activations.shape
        columns = grad_out.shape[1]
        rows, cols = features // count, columns // nodes
        half = count // 2
        levels = nodes.bit_length() - 1
        if cols % 128:
            grad_out = grad_out.reshape(tokens, nodes, cols).transpose(1, 0, 2)
        lines = -(-3 * nodes // 2 // 8) * 8
        hop = (2, nodes, half)
        dma = pltpu.SemaphoreType.DMA
        return pl.pallas_call(
            functools.partial(kernel, nodes, count),
            out_shape=jax.ShapeDtypeStruct((rows, cols), jnp.float32),
            in_specs=[pl.BlockSpec(memory_space=pl.ANY)] * 2,
            out_specs=pl.BlockSpec(memory_space=pltpu.VMEM),
            scratch_shapes=[
                pltpu.VMEM((tokens, features), jnp.bfloat16),
                pltpu.VMEM((features, tokens), jnp.bfloat16),
                pltpu.VMEM(grad_out.shape, jnp.bfloat16),
                pltpu.VMEM(hop + (rows, cols), jnp.bfloat16),
                pltpu.VMEM(hop + (rows, cols), jnp.bfloat16),
                pltpu.VMEM(hop + (16, 128), jnp.bfloat16),
                pltpu.VMEM(hop + (16, 128), jnp.bfloat16),
                pltpu.VMEM((rows, cols), jnp.float32),
                pltpu.VMEM((CHUNK, cols), jnp.float32),
                pltpu.VMEM((nodes, rows, cols), jnp.float32),
                pltpu.VMEM((nodes, rows, cols), jnp.float32),
                pltpu.VMEM((levels, 2, lines, 128), jnp.float32),
                pltpu.VMEM((levels, 2, max(nodes, count), lines, 128), jnp.float32),
                dma((Z_SIZE,)), dma((nodes,)),
                dma(hop), dma(hop), dma(hop), dma(hop),
                dma((nodes,)), dma((nodes,)),
                dma((levels, 2, max(nodes, count))), dma((levels, 2, max(nodes, count))),
            ],
            compiler_params=pltpu.CompilerParams(
                collective_id=0, has_side_effects=True, vmem_limit_bytes=60 * 2**20),
        )(activations, grad_out)

    in_specs = (P(("node", "fsdp"), None), P(("node", "fsdp"), None))
    return jax.shard_map(local, mesh=mesh, in_specs=in_specs, out_specs=P("fsdp", "node"), check_vma=False)
```

```python
import functools

import jax
import jax.numpy as jnp
from jax import lax
from jax.experimental import pallas as pl
from jax.experimental.pallas import tpu as pltpu
from jax.sharding import PartitionSpec as P

EPS = 1e-06
MESH = pl.DeviceIdType.MESH
TOP = 2.0**14
Z_SIZE = 4
CHUNK = 16


def ring_place(position, count):
    x_size = count // Z_SIZE
    inner = x_size - 1
    past = (position + count - Z_SIZE) // count
    rest = (position - Z_SIZE + count) % count
    line = rest // inner
    step = rest % inner
    odd = line % 2
    x = (1 - odd) * (1 + step) + odd * (x_size - 1 - step)
    z = Z_SIZE - 1 - line
    return past * (z * x_size + x) + (1 - past) * position * x_size


def ring_position(index, count):
    x_size = count // Z_SIZE
    inner = x_size - 1
    z = index // x_size
    x = index % x_size
    past = (x + inner) // x_size
    line = Z_SIZE - 1 - z
    odd = line % 2
    step = (1 - odd) * (x - 1) + odd * (x_size - 1 - x)
    return past * (Z_SIZE + line * inner + step) + (1 - past) * z


def encode(value, scale):
    x = value * scale
    square = x * x
    fourth = square * square
    eighth = fourth * fourth
    return jnp.where(x < 0, -eighth, eighth).astype(jnp.bfloat16)


def decode(code, top):
    y = code.astype(jnp.float32)
    root = lax.rsqrt(lax.rsqrt(jnp.maximum(jnp.abs(y), 1e-37)))
    value = root * lax.rsqrt(root) * (top * (1.0 / TOP))
    return jnp.where(y < 0, -value, value)


def kernel(
    nodes, count, a_ref, g_hbm, out_ref,
    raw, at_ref, g_ref, sent, came, sent_top, came_top, acc, peaks, own, gathered, sums_mine, sums_came,
    a_sem, g_sem, send_sem, recv_sem, top_send, top_recv, swap_send, swap_recv, sum_send, sum_recv,
):
    node = lax.axis_index("node")
    place = lax.axis_index("fsdp")
    rows, cols = acc.shape
    me = ring_position(place, count)
    right = ring_place((me + 1) % count, count)
    left = ring_place((me + count - 1) % count, count)
    half = count // 2

    x_size = count // Z_SIZE
    width = raw.shape[1] // Z_SIZE
    far_group = ring_place((me + half) % count, count) // x_size

    def pair_at(turn):
        return (node // 2 + 1 + turn) % (nodes // 2)

    def g_view(ref, block):
        if ref.ndim == 3:
            return ref.at[block]
        return ref.at[:, pl.ds(pl.multiple_of(block * cols, cols), cols)]

    def a_load(group):
        part = pl.ds(pl.multiple_of(group * width, 128), width)
        return pltpu.make_async_copy(a_ref.at[:, part], raw.at[:, part], a_sem.at[group])

    def g_load(block):
        return pltpu.make_async_copy(g_view(g_hbm, block), g_view(g_ref, block), g_sem.at[block])

    barrier = pltpu.get_barrier_semaphore()
    for k in range(1, count):
        pl.semaphore_signal(barrier, inc=1, device_id=(node, (place + k) % count), device_id_type=MESH)
    for k in range(1, nodes):
        pl.semaphore_signal(barrier, inc=1, device_id=((node + k) % nodes, place), device_id_type=MESH)
    a_load(far_group).start()
    for parity in range(2):
        g_load(2 * pair_at(0) + parity).start()
    for k in range(1, Z_SIZE):
        a_load((far_group + k) % Z_SIZE).start()

    @pl.loop(1, nodes // 2)
    def _(turn):
        for parity in range(2):
            g_load(2 * pair_at(turn) + parity).start()

    def transpose_group(group):
        a_load(group).wait()

        @pl.loop(0, width // 128)
        def _(i):
            part = pl.ds(pl.multiple_of(group * width + i * 128, 128), 128)
            at_ref[part, :] = raw[:, part].T

    transpose_group(far_group)
    pl.semaphore_wait(barrier, count + nodes - 2)

    def product(owner, block):
        mine = at_ref[pl.ds(pl.multiple_of(owner * rows, 16), rows), :]
        acc[...] = jnp.dot(mine, g_view(g_ref, block)[...], preferred_element_type=jnp.float32)

    def copies(side, block, step):
        target = (node, right * (1 - side) + left * side)
        data = pltpu.make_async_remote_copy(
            src_ref=sent.at[side, block, step], dst_ref=came.at[side, block, step],
            send_sem=send_sem.at[side, block, step], recv_sem=recv_sem.at[side, block, step],
            device_id=target, device_id_type=MESH)
        top = pltpu.make_async_remote_copy(
            src_ref=sent_top.at[side, block, step], dst_ref=came_top.at[side, block, step],
            send_sem=top_send.at[side, block, step], recv_sem=top_recv.at[side, block, step],
            device_id=target, device_id_type=MESH)
        return data, top

    def by_chunk(body, start=None):
        def step(i, carry):
            return body(pl.ds(pl.multiple_of(i * CHUNK, CHUNK), CHUNK), carry)

        return lax.fori_loop(0, rows // CHUNK, step, start, unroll=2)

    def arrived(side, block, step):
        data, top = copies(side, block, step)
        top.wait_recv()
        data.wait_recv()
        return came_top[side, block, step][0:1, 0:1].astype(jnp.float32)

    def hops(side, parity):
        return half if side == parity else count - 1 - half

    def send_on(side, parity, block, step):
        distance = hops(side, parity) - step
        far = (me + distance) % count if side == 0 else (me + count - distance) % count
        product(ring_place(far, count), block)

        @pl.when(step > 0)
        def _():
            top = arrived(side, block, step - 1)

            def add(part, peak):
                value = acc[part, :] + decode(came[side, block, step - 1, part, :], top)
                acc[part, :] = value
                return jnp.maximum(peak, jnp.abs(value))

            peaks[...] = by_chunk(add, jnp.zeros(peaks.shape, jnp.float32))

        @pl.when(step == 0)
        def _():
            peaks[...] = by_chunk(
                lambda part, peak: jnp.maximum(peak, jnp.abs(acc[part, :])), jnp.zeros(peaks.shape, jnp.float32))

        largest = jnp.maximum(jnp.max(peaks[...], axis=(0, 1), keepdims=True), 1e-30)
        tile = jnp.broadcast_to(largest, (16, 128)).astype(jnp.bfloat16)
        sent_top[side, block, step] = tile
        scale = TOP / tile[0:1, 0:1].astype(jnp.float32)

        def code(part, carry):
            sent[side, block, step, part, :] = encode(acc[part, :], scale)

        by_chunk(code)
        data, top = copies(side, block, step)
        top.start()
        data.start()

    def swap(block):
        return pltpu.make_async_remote_copy(
            src_ref=own.at[block], dst_ref=gathered.at[node],
            send_sem=swap_send.at[block], recv_sem=swap_recv.at[node],
            device_id=(block, place), device_id_type=MESH)

    def prepare(parity, block):
        product(place, block)
        top = arrived(1 - parity, block, half - 2)

        def add(part, carry):
            own[block, part, :] = acc[part, :] + decode(came[1 - parity, block, half - 2, part, :], top)

        by_chunk(add)

    def finish(parity, block):
        top = arrived(parity, block, half - 1)

        def total(part):
            return own[block, part, :] + decode(came[parity, block, half - 1, part, :], top)

        @pl.when(block != node)
        def _():
            def store(part, carry):
                own[block, part, :] = total(part)

            by_chunk(store)
            swap(block).start()

        @pl.when(block == node)
        def _():
            def store(part, carry):
                gathered[block, part, :] = total(part)

            by_chunk(store)

    def finish_pair(turn):
        for parity in range(2):
            prepare(parity, 2 * pair_at(turn) + parity)
        for parity in (1 - node % 2, node % 2):
            finish(parity, 2 * pair_at(turn) + parity)

    @pl.loop(0, nodes // 2)
    def _(turn):
        pair = pair_at(turn)
        for parity in range(2):
            g_load(2 * pair + parity).wait()

        @pl.loop(0, half)
        def _(step):
            for side in range(2):
                send_on(side, side, 2 * pair + side, step)

            @pl.when((turn == 0) & (step == 0))
            def _():
                for k in range(1, Z_SIZE):
                    transpose_group((far_group + k) % Z_SIZE)

            @pl.when(step < half - 1)
            def _():
                for side in range(2):
                    send_on(side, 1 - side, 2 * pair + 1 - side, step)

            @pl.when((step == 0) & (turn > 0))
            def _():
                finish_pair(turn - 1)

    finish_pair(nodes // 2 - 1)

    @pl.loop(1, nodes)
    def _(k):
        other = (node + k) % nodes
        pltpu.make_async_remote_copy(
            src_ref=own.at[other], dst_ref=gathered.at[other],
            send_sem=swap_send.at[other], recv_sem=swap_recv.at[other],
            device_id=(other, place), device_id_type=MESH).wait_recv()

    def exchange(level, stage, size):
        def copy(k):
            far = (node, (place + k) % count) if stage == 0 else ((node + k) % nodes, place)
            return pltpu.make_async_remote_copy(
                src_ref=sums_mine.at[level, stage], dst_ref=sums_came.at[level, stage, k],
                send_sem=sum_send.at[level, stage, k], recv_sem=sum_recv.at[level, stage, k],
                device_id=far, device_id_type=MESH)

        for k in range(1, size):
            copy(k).start()
        total = sums_mine[level, stage]
        for k in range(1, size):
            copy(k).wait_recv()
            total = total + sums_came[level, stage, k]
        for k in range(1, size):
            copy(k).wait_send()
        return total

    def whole_sum(value):
        return jnp.sum(jnp.sum(value, axis=0, keepdims=True), axis=1, keepdims=True)

    def fold(value):
        if cols % 128:
            return value
        return sum(value[:, i : i + 128] for i in range(0, cols, 128))

    def reduce_all(level, pairs_of, number):
        def step(i, sums):
            part = pl.ds(pl.multiple_of(i * 8, 8), 8)
            return tuple(t + fold(a * b) for t, (a, b) in zip(sums, pairs_of(part)))

        start = jnp.zeros((8, cols if cols % 128 else 128), jnp.float32)
        sums = lax.fori_loop(0, rows // 8, step, (start,) * number, unroll=2)
        tile = jnp.zeros(sums_mine.shape[2:], jnp.float32)
        line = lax.broadcasted_iota(jnp.int32, tile.shape, 0)
        for i, term in enumerate(sums):
            tile = jnp.where(line == i, whole_sum(term), tile)
        sums_mine[level, 0] = tile
        sums_mine[level, 1] = exchange(level, 0, count)
        total = exchange(level, 1, nodes)
        return [total[i : i + 1, 0:1] for i in range(number)]

    def coefs(inner, first_sq, second_sq):
        return 1.0 - inner / (2.0 * (first_sq + EPS)), 1.0 - inner / (2.0 * (second_sq + EPS))

    def one_level(level, left):
        def products(part):
            for j in range(left):
                first, second = gathered[j, part, :], gathered[j + left, part, :]
                yield from ((first, second), (first, first), (second, second))

        sums = reduce_all(level, products, 3 * left)
        for j in range(left):
            coef_first, coef_second = coefs(*sums[3 * j : 3 * j + 3])

            def mix(part, carry):
                mixed = coef_first * gathered[j, part, :] + coef_second * gathered[j + left, part, :]
                if left == 1:
                    out_ref[part, :] = mixed
                else:
                    gathered[j, part, :] = mixed

            by_chunk(mix)

    def two_levels(level):
        def products(part):
            bases = []
            for j in range(2):
                first, second = gathered[j, part, :], gathered[j + 2, part, :]
                both = first + second
                bases.append((first, second, both))
                yield from ((first, second), (first, first), (second, second), (both, both), (both, first - second))
            for left in bases[0]:
                for right in bases[1]:
                    yield left, right

        sums = reduce_all(level, products, 19)
        pairs = []
        for j in range(2):
            inner, first_sq, second_sq, both_sq, cross = sums[5 * j : 5 * j + 5]
            first, second = coefs(inner, first_sq, second_sq)
            cancels = both_sq < 0.25 * (first_sq + second_sq)
            mean = 0.5 * (first + second)
            gap = 0.25 * (inner / (first_sq + EPS)) * (cross / (second_sq + EPS))
            plain = first * (first * first_sq) + 2.0 * (first * (second * inner)) + second * (second * second_sq)
            apart_sq = first_sq + second_sq - 2.0 * inner
            by_sum = mean * (mean * both_sq) + 2.0 * (mean * (gap * cross)) + gap * (gap * apart_sq)
            weights = (jnp.where(cancels, gap, first), jnp.where(cancels, -gap, second), mean)
            pairs.append((first, second, jnp.where(cancels, by_sum, plain), cancels, weights))
        inner = jnp.zeros((1, 1), jnp.float32)
        for i in range(3):
            for k in range(3):
                term = pairs[0][4][i] * (pairs[1][4][k] * sums[10 + 3 * i + k])
                if i == 2:
                    term = jnp.where(pairs[0][3], term, 0.0)
                if k == 2:
                    term = jnp.where(pairs[1][3], term, 0.0)
                inner = inner + term
        low, high = coefs(inner, pairs[0][2], pairs[1][2])

        def mix(part, carry):
            below = pairs[0][0] * gathered[0, part, :] + pairs[0][1] * gathered[2, part, :]
            above = pairs[1][0] * gathered[1, part, :] + pairs[1][1] * gathered[3, part, :]
            out_ref[part, :] = low * below + high * above

        by_chunk(mix)

    level, matrices = 0, nodes
    while matrices > 1:
        if matrices == 4:
            two_levels(level)
            break
        matrices //= 2
        one_level(level, matrices)
        level += 1

    @pl.loop(1, nodes)
    def _(k):
        swap((node + k) % nodes).wait_send()

    @pl.loop(0, nodes // 2)
    def _(pair):
        for parity in range(2):
            for side in range(2):
                @pl.loop(0, hops(side, parity))
                def _(step):
                    data, top = copies(side, 2 * pair + parity, step)
                    top.wait_send()
                    data.wait_send()


def solution(mesh):
    nodes, count = mesh.shape["node"], mesh.shape["fsdp"]

    def local(activations, grad_out):
        tokens, features = activations.shape
        columns = grad_out.shape[1]
        rows, cols = features // count, columns // nodes
        half = count // 2
        levels = nodes.bit_length() - 1
        if cols % 128:
            grad_out = grad_out.reshape(tokens, nodes, cols).transpose(1, 0, 2)
        lines = max(24, -(-3 * nodes // 2 // 8) * 8)
        hop = (2, nodes, half)
        dma = pltpu.SemaphoreType.DMA
        return pl.pallas_call(
            functools.partial(kernel, nodes, count),
            out_shape=jax.ShapeDtypeStruct((rows, cols), jnp.float32),
            in_specs=[pl.BlockSpec(memory_space=pl.ANY)] * 2,
            out_specs=pl.BlockSpec(memory_space=pltpu.VMEM),
            scratch_shapes=[
                pltpu.VMEM((tokens, features), jnp.bfloat16),
                pltpu.VMEM((features, tokens), jnp.bfloat16),
                pltpu.VMEM(grad_out.shape, jnp.bfloat16),
                pltpu.VMEM(hop + (rows, cols), jnp.bfloat16),
                pltpu.VMEM(hop + (rows, cols), jnp.bfloat16),
                pltpu.VMEM(hop + (16, 128), jnp.bfloat16),
                pltpu.VMEM(hop + (16, 128), jnp.bfloat16),
                pltpu.VMEM((rows, cols), jnp.float32),
                pltpu.VMEM((CHUNK, cols), jnp.float32),
                pltpu.VMEM((nodes, rows, cols), jnp.float32),
                pltpu.VMEM((nodes, rows, cols), jnp.float32),
                pltpu.VMEM((levels, 2, lines, 128), jnp.float32),
                pltpu.VMEM((levels, 2, max(nodes, count), lines, 128), jnp.float32),
                dma((Z_SIZE,)), dma((nodes,)),
                dma(hop), dma(hop), dma(hop), dma(hop),
                dma((nodes,)), dma((nodes,)),
                dma((levels, 2, max(nodes, count))), dma((levels, 2, max(nodes, count))),
            ],
            compiler_params=pltpu.CompilerParams(
                collective_id=0, has_side_effects=True, vmem_limit_bytes=60 * 2**20),
        )(activations, grad_out)

    in_specs = (P(("node", "fsdp"), None), P(("node", "fsdp"), None))
    return jax.shard_map(local, mesh=mesh, in_specs=in_specs, out_specs=P("fsdp", "node"), check_vma=False)
```

```python
import functools

import jax
import jax.numpy as jnp
from jax import lax
from jax.experimental import pallas as pl
from jax.experimental.pallas import tpu as pltpu
from jax.sharding import PartitionSpec as P

EPS = 1e-06
MESH = pl.DeviceIdType.MESH
TOP = 2.0**14
Z_SIZE = 4
CHUNK = 16


def ring_place(position, count):
    x_size = count // Z_SIZE
    inner = x_size - 1
    past = (position + count - Z_SIZE) // count
    rest = (position - Z_SIZE + count) % count
    line = rest // inner
    step = rest % inner
    odd = line % 2
    x = (1 - odd) * (1 + step) + odd * (x_size - 1 - step)
    z = Z_SIZE - 1 - line
    return past * (z * x_size + x) + (1 - past) * position * x_size


def ring_position(index, count):
    x_size = count // Z_SIZE
    inner = x_size - 1
    z = index // x_size
    x = index % x_size
    past = (x + inner) // x_size
    line = Z_SIZE - 1 - z
    odd = line % 2
    step = (1 - odd) * (x - 1) + odd * (x_size - 1 - x)
    return past * (Z_SIZE + line * inner + step) + (1 - past) * z


def encode(value, scale):
    x = value * scale
    square = x * x
    fourth = square * square
    eighth = fourth * fourth
    return jnp.where(x < 0, -eighth, eighth).astype(jnp.bfloat16)


def decode(code, top):
    y = code.astype(jnp.float32)
    root = lax.rsqrt(lax.rsqrt(jnp.maximum(jnp.abs(y), 1e-37)))
    value = root * lax.rsqrt(root) * (top * (1.0 / TOP))
    return jnp.where(y < 0, -value, value)


def kernel(
    nodes, count, a_ref, g_hbm, out_ref,
    raw, at_ref, g_ref, sent, came, sent_top, came_top, acc, peaks, own, gathered, sums_mine, sums_came,
    a_sem, g_sem, send_sem, recv_sem, top_send, top_recv, swap_send, swap_recv, sum_send, sum_recv,
):
    node = lax.axis_index("node")
    place = lax.axis_index("fsdp")
    rows, cols = acc.shape
    me = ring_position(place, count)
    right = ring_place((me + 1) % count, count)
    left = ring_place((me + count - 1) % count, count)
    half = count // 2

    x_size = count // Z_SIZE
    width = raw.shape[1] // Z_SIZE
    far_group = ring_place((me + half) % count, count) // x_size

    def pair_at(turn):
        return (node // 2 + 1 + turn) % (nodes // 2)

    def g_view(ref, block):
        if ref.ndim == 3:
            return ref.at[block]
        return ref.at[:, pl.ds(pl.multiple_of(block * cols, cols), cols)]

    def a_load(group):
        part = pl.ds(pl.multiple_of(group * width, 128), width)
        return pltpu.make_async_copy(a_ref.at[:, part], raw.at[:, part], a_sem.at[group])

    def g_load(block):
        return pltpu.make_async_copy(g_view(g_hbm, block), g_view(g_ref, block), g_sem.at[block])

    barrier = pltpu.get_barrier_semaphore()
    for k in range(1, count):
        pl.semaphore_signal(barrier, inc=1, device_id=(node, (place + k) % count), device_id_type=MESH)
    for k in range(1, nodes):
        pl.semaphore_signal(barrier, inc=1, device_id=((node + k) % nodes, place), device_id_type=MESH)
    a_load(far_group).start()
    for parity in range(2):
        g_load(2 * pair_at(0) + parity).start()
    for k in range(1, Z_SIZE):
        a_load((far_group + k) % Z_SIZE).start()

    @pl.loop(1, nodes // 2)
    def _(turn):
        for parity in range(2):
            g_load(2 * pair_at(turn) + parity).start()

    def transpose_group(group):
        a_load(group).wait()

        @pl.loop(0, width // 128)
        def _(i):
            part = pl.ds(pl.multiple_of(group * width + i * 128, 128), 128)
            at_ref[part, :] = raw[:, part].T

    transpose_group(far_group)
    pl.semaphore_wait(barrier, count + nodes - 2)

    def product(owner, block):
        mine = at_ref[pl.ds(pl.multiple_of(owner * rows, 16), rows), :]
        acc[...] = jnp.dot(mine, g_view(g_ref, block)[...], preferred_element_type=jnp.float32)

    def copies(side, block, step):
        target = (node, right * (1 - side) + left * side)
        data = pltpu.make_async_remote_copy(
            src_ref=sent.at[side, block, step], dst_ref=came.at[side, block, step],
            send_sem=send_sem.at[side, block, step], recv_sem=recv_sem.at[side, block, step],
            device_id=target, device_id_type=MESH)
        top = pltpu.make_async_remote_copy(
            src_ref=sent_top.at[side, block, step], dst_ref=came_top.at[side, block, step],
            send_sem=top_send.at[side, block, step], recv_sem=top_recv.at[side, block, step],
            device_id=target, device_id_type=MESH)
        return data, top

    def by_chunk(body, start=None):
        def step(i, carry):
            return body(pl.ds(pl.multiple_of(i * CHUNK, CHUNK), CHUNK), carry)

        return lax.fori_loop(0, rows // CHUNK, step, start, unroll=5)

    def arrived(side, block, step):
        data, top = copies(side, block, step)
        top.wait_recv()
        data.wait_recv()
        return came_top[side, block, step][0:1, 0:1].astype(jnp.float32)

    def hops(side, parity):
        return half if side == parity else count - 1 - half

    def send_on(side, parity, block, step):
        distance = hops(side, parity) - step
        far = (me + distance) % count if side == 0 else (me + count - distance) % count
        product(ring_place(far, count), block)

        @pl.when(step > 0)
        def _():
            top = arrived(side, block, step - 1)

            def add(part, peak):
                value = acc[part, :] + decode(came[side, block, step - 1, part, :], top)
                acc[part, :] = value
                return jnp.maximum(peak, jnp.abs(value))

            peaks[...] = by_chunk(add, jnp.zeros(peaks.shape, jnp.float32))

        @pl.when(step == 0)
        def _():
            peaks[...] = by_chunk(
                lambda part, peak: jnp.maximum(peak, jnp.abs(acc[part, :])), jnp.zeros(peaks.shape, jnp.float32))

        largest = jnp.maximum(jnp.max(peaks[...], axis=(0, 1), keepdims=True), 1e-30)
        tile = jnp.broadcast_to(largest, (16, 128)).astype(jnp.bfloat16)
        sent_top[side, block, step] = tile
        scale = TOP / tile[0:1, 0:1].astype(jnp.float32)

        def code(part, carry):
            sent[side, block, step, part, :] = encode(acc[part, :], scale)

        by_chunk(code)
        data, top = copies(side, block, step)
        top.start()
        data.start()

    def swap(block):
        return pltpu.make_async_remote_copy(
            src_ref=own.at[block], dst_ref=gathered.at[node],
            send_sem=swap_send.at[block], recv_sem=swap_recv.at[node],
            device_id=(block, place), device_id_type=MESH)

    def prepare(parity, block):
        product(place, block)
        top = arrived(1 - parity, block, half - 2)

        def add(part, carry):
            own[block, part, :] = acc[part, :] + decode(came[1 - parity, block, half - 2, part, :], top)

        by_chunk(add)

    def finish(parity, block):
        top = arrived(parity, block, half - 1)

        def total(part):
            return own[block, part, :] + decode(came[parity, block, half - 1, part, :], top)

        @pl.when(block != node)
        def _():
            def store(part, carry):
                own[block, part, :] = total(part)

            by_chunk(store)
            swap(block).start()

        @pl.when(block == node)
        def _():
            def store(part, carry):
                gathered[block, part, :] = total(part)

            by_chunk(store)

    def finish_pair(turn):
        for parity in range(2):
            prepare(parity, 2 * pair_at(turn) + parity)
        for parity in (1 - node % 2, node % 2):
            finish(parity, 2 * pair_at(turn) + parity)

    @pl.loop(0, nodes // 2)
    def _(turn):
        pair = pair_at(turn)
        for parity in range(2):
            g_load(2 * pair + parity).wait()

        @pl.loop(0, half)
        def _(step):
            for side in range(2):
                send_on(side, side, 2 * pair + side, step)

            @pl.when((turn == 0) & (step == 0))
            def _():
                for k in (1, Z_SIZE - 1):
                    transpose_group((far_group + k) % Z_SIZE)

            @pl.when(step < half - 1)
            def _():
                for side in range(2):
                    send_on(side, 1 - side, 2 * pair + 1 - side, step)

            @pl.when((turn == 0) & (step == 0))
            def _():
                for k in range(2, Z_SIZE - 1):
                    transpose_group((far_group + k) % Z_SIZE)

            @pl.when((step == 0) & (turn > 0))
            def _():
                finish_pair(turn - 1)

    finish_pair(nodes // 2 - 1)

    @pl.loop(1, nodes)
    def _(k):
        other = (node + k) % nodes
        pltpu.make_async_remote_copy(
            src_ref=own.at[other], dst_ref=gathered.at[other],
            send_sem=swap_send.at[other], recv_sem=swap_recv.at[other],
            device_id=(other, place), device_id_type=MESH).wait_recv()

    def exchange(level, stage, size):
        def copy(k):
            far = (node, (place + k) % count) if stage == 0 else ((node + k) % nodes, place)
            return pltpu.make_async_remote_copy(
                src_ref=sums_mine.at[level, stage], dst_ref=sums_came.at[level, stage, k],
                send_sem=sum_send.at[level, stage, k], recv_sem=sum_recv.at[level, stage, k],
                device_id=far, device_id_type=MESH)

        for k in range(1, size):
            copy(k).start()
        total = sums_mine[level, stage]
        for k in range(1, size):
            copy(k).wait_recv()
            total = total + sums_came[level, stage, k]
        for k in range(1, size):
            copy(k).wait_send()
        return total

    def whole_sum(value):
        return jnp.sum(jnp.sum(value, axis=0, keepdims=True), axis=1, keepdims=True)

    def fold(value):
        if cols % 128:
            return value
        return sum(value[:, i : i + 128] for i in range(0, cols, 128))

    def reduce_all(level, pairs_of, number):
        def step(i, sums):
            part = pl.ds(pl.multiple_of(i * 8, 8), 8)
            return tuple(t + fold(a * b) for t, (a, b) in zip(sums, pairs_of(part)))

        start = jnp.zeros((8, cols if cols % 128 else 128), jnp.float32)
        sums = lax.fori_loop(0, rows // 8, step, (start,) * number, unroll=2)
        tile = jnp.zeros(sums_mine.shape[2:], jnp.float32)
        line = lax.broadcasted_iota(jnp.int32, tile.shape, 0)
        for i, term in enumerate(sums):
            tile = jnp.where(line == i, whole_sum(term), tile)
        sums_mine[level, 0] = tile
        sums_mine[level, 1] = exchange(level, 0, count)
        total = exchange(level, 1, nodes)
        return [total[i : i + 1, 0:1] for i in range(number)]

    def coefs(inner, first_sq, second_sq):
        return 1.0 - inner / (2.0 * (first_sq + EPS)), 1.0 - inner / (2.0 * (second_sq + EPS))

    def one_level(level, left):
        def products(part):
            for j in range(left):
                first, second = gathered[j, part, :], gathered[j + left, part, :]
                yield from ((first, second), (first, first), (second, second))

        sums = reduce_all(level, products, 3 * left)
        for j in range(left):
            coef_first, coef_second = coefs(*sums[3 * j : 3 * j + 3])

            def mix(part, carry):
                terms = coef_first * gathered[j, part, :], coef_second * gathered[j + left, part, :]
                if left == 1:
                    out_ref[0, part, :], out_ref[1, part, :] = terms
                else:
                    gathered[j, part, :] = terms[0] + terms[1]

            by_chunk(mix)

    def two_levels(level):
        def products(part):
            bases = []
            for j in range(2):
                first, second = gathered[j, part, :], gathered[j + 2, part, :]
                both = first + second
                bases.append((first, second, both))
                yield from ((first, second), (first, first), (second, second), (both, both), (both, first - second))
            for left in bases[0]:
                for right in bases[1]:
                    yield left, right

        sums = reduce_all(level, products, 19)
        pairs = []
        for j in range(2):
            inner, first_sq, second_sq, both_sq, cross = sums[5 * j : 5 * j + 5]
            first, second = coefs(inner, first_sq, second_sq)
            cancels = both_sq < 0.25 * (first_sq + second_sq)
            mean = 0.5 * (first + second)
            gap = 0.25 * (inner / (first_sq + EPS)) * (cross / (second_sq + EPS))
            plain = first * (first * first_sq) + 2.0 * (first * (second * inner)) + second * (second * second_sq)
            apart_sq = first_sq + second_sq - 2.0 * inner
            by_sum = mean * (mean * both_sq) + 2.0 * (mean * (gap * cross)) + gap * (gap * apart_sq)
            weights = (jnp.where(cancels, gap, first), jnp.where(cancels, -gap, second), mean)
            pairs.append((first, second, jnp.where(cancels, by_sum, plain), cancels, weights))
        inner = jnp.zeros((1, 1), jnp.float32)
        for i in range(3):
            for k in range(3):
                term = pairs[0][4][i] * (pairs[1][4][k] * sums[10 + 3 * i + k])
                if i == 2:
                    term = jnp.where(pairs[0][3], term, 0.0)
                if k == 2:
                    term = jnp.where(pairs[1][3], term, 0.0)
                inner = inner + term
        low, high = coefs(inner, pairs[0][2], pairs[1][2])

        def mix(part, carry):
            below = pairs[0][0] * gathered[0, part, :] + pairs[0][1] * gathered[2, part, :]
            above = pairs[1][0] * gathered[1, part, :] + pairs[1][1] * gathered[3, part, :]
            out_ref[0, part, :] = low * below
            out_ref[1, part, :] = high * above

        by_chunk(mix)

    level, matrices = 0, nodes
    while matrices > 1:
        if matrices == 4:
            two_levels(level)
            break
        matrices //= 2
        one_level(level, matrices)
        level += 1

    @pl.loop(1, nodes)
    def _(k):
        swap((node + k) % nodes).wait_send()

    @pl.loop(0, nodes // 2)
    def _(pair):
        for parity in range(2):
            for side in range(2):
                @pl.loop(0, hops(side, parity))
                def _(step):
                    data, top = copies(side, 2 * pair + parity, step)
                    top.wait_send()
                    data.wait_send()


def solution(mesh):
    nodes, count = mesh.shape["node"], mesh.shape["fsdp"]

    def local(activations, grad_out):
        tokens, features = activations.shape
        columns = grad_out.shape[1]
        rows, cols = features // count, columns // nodes
        half = count // 2
        levels = nodes.bit_length() - 1
        if cols % 128:
            grad_out = grad_out.reshape(tokens, nodes, cols).transpose(1, 0, 2)
        lines = max(24, -(-3 * nodes // 2 // 8) * 8)
        hop = (2, nodes, half)
        dma = pltpu.SemaphoreType.DMA
        terms = pl.pallas_call(
            functools.partial(kernel, nodes, count),
            out_shape=jax.ShapeDtypeStruct((2, rows, cols), jnp.float32),
            in_specs=[pl.BlockSpec(memory_space=pl.ANY)] * 2,
            out_specs=pl.BlockSpec(memory_space=pltpu.VMEM),
            scratch_shapes=[
                pltpu.VMEM((tokens, features), jnp.bfloat16),
                pltpu.VMEM((features, tokens), jnp.bfloat16),
                pltpu.VMEM(grad_out.shape, jnp.bfloat16),
                pltpu.VMEM(hop + (rows, cols), jnp.bfloat16),
                pltpu.VMEM(hop + (rows, cols), jnp.bfloat16),
                pltpu.VMEM(hop + (16, 128), jnp.bfloat16),
                pltpu.VMEM(hop + (16, 128), jnp.bfloat16),
                pltpu.VMEM((rows, cols), jnp.float32),
                pltpu.VMEM((CHUNK, cols), jnp.float32),
                pltpu.VMEM((nodes, rows, cols), jnp.float32),
                pltpu.VMEM((nodes, rows, cols), jnp.float32),
                pltpu.VMEM((levels, 2, lines, 128), jnp.float32),
                pltpu.VMEM((levels, 2, max(nodes, count), lines, 128), jnp.float32),
                dma((Z_SIZE,)), dma((nodes,)),
                dma(hop), dma(hop), dma(hop), dma(hop),
                dma((nodes,)), dma((nodes,)),
                dma((levels, 2, max(nodes, count))), dma((levels, 2, max(nodes, count))),
            ],
            compiler_params=pltpu.CompilerParams(
                collective_id=0, has_side_effects=True, vmem_limit_bytes=60 * 2**20),
        )(activations, grad_out)
        return terms[0] + terms[1]

    in_specs = (P(("node", "fsdp"), None), P(("node", "fsdp"), None))
    return jax.shard_map(local, mesh=mesh, in_specs=in_specs, out_specs=P("fsdp", "node"), check_vma=False)
```

```python
import functools

import jax
import jax.numpy as jnp
from jax import lax
from jax.experimental import pallas as pl
from jax.experimental.pallas import tpu as pltpu
from jax.sharding import PartitionSpec as P

EPS = 1e-06
MESH = pl.DeviceIdType.MESH
TOP = 2.0**14
Z_SIZE = 4
CHUNK = 16


def ring_place(position, count):
    x_size = count // Z_SIZE
    inner = x_size - 1
    past = (position + count - Z_SIZE) // count
    rest = (position - Z_SIZE + count) % count
    line = rest // inner
    step = rest % inner
    odd = line % 2
    x = (1 - odd) * (1 + step) + odd * (x_size - 1 - step)
    z = Z_SIZE - 1 - line
    return past * (z * x_size + x) + (1 - past) * position * x_size


def ring_position(index, count):
    x_size = count // Z_SIZE
    inner = x_size - 1
    z = index // x_size
    x = index % x_size
    past = (x + inner) // x_size
    line = Z_SIZE - 1 - z
    odd = line % 2
    step = (1 - odd) * (x - 1) + odd * (x_size - 1 - x)
    return past * (Z_SIZE + line * inner + step) + (1 - past) * z


def encode(value, scale):
    x = value * scale
    square = x * x
    fourth = square * square
    eighth = fourth * fourth
    return jnp.where(x < 0, -eighth, eighth).astype(jnp.bfloat16)


def decode(code, top):
    y = code.astype(jnp.float32)
    root = lax.rsqrt(lax.rsqrt(jnp.maximum(jnp.abs(y), 1e-37)))
    value = root * lax.rsqrt(root) * (top * (1.0 / TOP))
    return jnp.where(y < 0, -value, value)


def kernel(
    nodes, count, a_ref, g_hbm, out_ref,
    raw, at_ref, g_ref, sent, came, sent_top, came_top, acc, peaks, own, gathered, sums_mine, sums_came,
    a_sem, g_sem, send_sem, recv_sem, top_send, top_recv, swap_send, swap_recv, sum_send, sum_recv,
):
    node = lax.axis_index("node")
    place = lax.axis_index("fsdp")
    rows, cols = acc.shape
    pieces = swap_send.shape[1]
    size = rows // pieces
    me = ring_position(place, count)
    right = ring_place((me + 1) % count, count)
    left = ring_place((me + count - 1) % count, count)
    half = count // 2

    x_size = count // Z_SIZE
    width = raw.shape[1] // Z_SIZE
    far_group = ring_place((me + half) % count, count) // x_size

    def pair_at(turn):
        return (node // 2 + 1 + turn) % (nodes // 2)

    def g_view(ref, block):
        if ref.ndim == 3:
            return ref.at[block]
        return ref.at[:, pl.ds(pl.multiple_of(block * cols, cols), cols)]

    def a_load(group):
        part = pl.ds(pl.multiple_of(group * width, 128), width)
        return pltpu.make_async_copy(a_ref.at[:, part], raw.at[:, part], a_sem.at[group])

    def g_load(block):
        return pltpu.make_async_copy(g_view(g_hbm, block), g_view(g_ref, block), g_sem.at[block])

    barrier = pltpu.get_barrier_semaphore()
    for k in range(1, count):
        pl.semaphore_signal(barrier, inc=1, device_id=(node, (place + k) % count), device_id_type=MESH)
    for k in range(1, nodes):
        pl.semaphore_signal(barrier, inc=1, device_id=((node + k) % nodes, place), device_id_type=MESH)
    a_load(far_group).start()
    for parity in range(2):
        g_load(2 * pair_at(0) + parity).start()
    for k in range(1, Z_SIZE):
        a_load((far_group + k) % Z_SIZE).start()

    @pl.loop(1, nodes // 2)
    def _(turn):
        for parity in range(2):
            g_load(2 * pair_at(turn) + parity).start()

    def transpose_group(group):
        a_load(group).wait()

        @pl.loop(0, width // 128)
        def _(i):
            part = pl.ds(pl.multiple_of(group * width + i * 128, 128), 128)
            at_ref[part, :] = raw[:, part].T

    transpose_group(far_group)
    pl.semaphore_wait(barrier, count + nodes - 2)

    def product(owner, block):
        mine = at_ref[pl.ds(pl.multiple_of(owner * rows, 16), rows), :]
        acc[...] = jnp.dot(mine, g_view(g_ref, block)[...], preferred_element_type=jnp.float32)

    def copies(side, block, step):
        target = (node, right * (1 - side) + left * side)
        data = pltpu.make_async_remote_copy(
            src_ref=sent.at[side, block, step], dst_ref=came.at[side, block, step],
            send_sem=send_sem.at[side, block, step], recv_sem=recv_sem.at[side, block, step],
            device_id=target, device_id_type=MESH)
        top = pltpu.make_async_remote_copy(
            src_ref=sent_top.at[side, block, step], dst_ref=came_top.at[side, block, step],
            send_sem=top_send.at[side, block, step], recv_sem=top_recv.at[side, block, step],
            device_id=target, device_id_type=MESH)
        return data, top

    def by_chunk(body, start=None, first=0, number=rows):
        def step(i, carry):
            return body(pl.ds(pl.multiple_of(first + i * CHUNK, CHUNK), CHUNK), carry)

        return lax.fori_loop(0, number // CHUNK, step, start, unroll=5)

    def arrived(side, block, step):
        data, top = copies(side, block, step)
        top.wait_recv()
        data.wait_recv()
        return came_top[side, block, step][0:1, 0:1].astype(jnp.float32)

    def hops(side, parity):
        return half if side == parity else count - 1 - half

    def send_on(side, parity, block, step):
        distance = hops(side, parity) - step
        far = (me + distance) % count if side == 0 else (me + count - distance) % count
        product(ring_place(far, count), block)

        @pl.when(step > 0)
        def _():
            top = arrived(side, block, step - 1)

            def add(part, peak):
                value = acc[part, :] + decode(came[side, block, step - 1, part, :], top)
                acc[part, :] = value
                return jnp.maximum(peak, jnp.abs(value))

            peaks[...] = by_chunk(add, jnp.zeros(peaks.shape, jnp.float32))

        @pl.when(step == 0)
        def _():
            peaks[...] = by_chunk(
                lambda part, peak: jnp.maximum(peak, jnp.abs(acc[part, :])), jnp.zeros(peaks.shape, jnp.float32))

        largest = jnp.maximum(jnp.max(peaks[...], axis=(0, 1), keepdims=True), 1e-30)
        tile = jnp.broadcast_to(largest, (16, 128)).astype(jnp.bfloat16)
        sent_top[side, block, step] = tile
        scale = TOP / tile[0:1, 0:1].astype(jnp.float32)

        def code(part, carry):
            sent[side, block, step, part, :] = encode(acc[part, :], scale)

        by_chunk(code)
        data, top = copies(side, block, step)
        top.start()
        data.start()

    def swap(block, piece, sender):
        part = pl.ds(pl.multiple_of(piece * size, 8), size)
        return pltpu.make_async_remote_copy(
            src_ref=own.at[block, part], dst_ref=gathered.at[sender, part],
            send_sem=swap_send.at[block, piece], recv_sem=swap_recv.at[sender, piece],
            device_id=(block, place), device_id_type=MESH)

    def prepare(parity, block):
        product(place, block)
        top = arrived(1 - parity, block, half - 2)

        def add(part, carry):
            own[block, part, :] = acc[part, :] + decode(came[1 - parity, block, half - 2, part, :], top)

        by_chunk(add)

    def finish(parity, block, send):
        top = arrived(parity, block, half - 1)

        def total(part):
            return own[block, part, :] + decode(came[parity, block, half - 1, part, :], top)

        @pl.when(block != node)
        def _():
            def store(part, carry):
                own[block, part, :] = total(part)

            for piece in range(pieces):
                by_chunk(store, None, piece * size, size)
                if send:
                    swap(block, piece, node).start()

        @pl.when(block == node)
        def _():
            def store(part, carry):
                gathered[block, part, :] = total(part)

            by_chunk(store)

    def finish_pair(turn, send):
        for parity in range(2):
            prepare(parity, 2 * pair_at(turn) + parity)
        for parity in (1 - node % 2, node % 2):
            finish(parity, 2 * pair_at(turn) + parity, send)

    @pl.loop(0, nodes // 2)
    def _(turn):
        pair = pair_at(turn)
        for parity in range(2):
            g_load(2 * pair + parity).wait()

        @pl.loop(0, half)
        def _(step):
            for side in range(2):
                send_on(side, side, 2 * pair + side, step)

            @pl.when((turn == 0) & (step == 0))
            def _():
                for k in (1, Z_SIZE - 1):
                    transpose_group((far_group + k) % Z_SIZE)

            @pl.when(step < half - 1)
            def _():
                for side in range(2):
                    send_on(side, 1 - side, 2 * pair + 1 - side, step)

            @pl.when((turn == 0) & (step == 0))
            def _():
                for k in range(2, Z_SIZE - 1):
                    transpose_group((far_group + k) % Z_SIZE)

            @pl.when((step == 0) & (turn > 0))
            def _():
                finish_pair(turn - 1, False)

            @pl.when((turn > 0) & (step < pieces))
            def _():
                for parity in range(2):
                    swap(2 * pair_at(turn - 1) + parity, step, node).start()

    finish_pair(nodes // 2 - 1, True)

    def exchange(level, stage, members):
        def copy(k):
            far = (node, (place + k) % count) if stage == 0 else ((node + k) % nodes, place)
            return pltpu.make_async_remote_copy(
                src_ref=sums_mine.at[level, stage], dst_ref=sums_came.at[level, stage, k],
                send_sem=sum_send.at[level, stage, k], recv_sem=sum_recv.at[level, stage, k],
                device_id=far, device_id_type=MESH)

        for k in range(1, members):
            copy(k).start()
        total = sums_mine[level, stage]
        for k in range(1, members):
            copy(k).wait_recv()
            total = total + sums_came[level, stage, k]
        for k in range(1, members):
            copy(k).wait_send()
        return total

    def whole_sum(value):
        return jnp.sum(jnp.sum(value, axis=0, keepdims=True), axis=1, keepdims=True)

    def fold(value):
        if cols % 128:
            return value
        return sum(value[:, i : i + 128] for i in range(0, cols, 128))

    def reduce_all(level, pairs_of, number):
        def step(i, sums):
            part = pl.ds(pl.multiple_of(i * 8, 8), 8)
            return tuple(t + fold(a * b) for t, (a, b) in zip(sums, pairs_of(part)))

        sums = (jnp.zeros((8, cols if cols % 128 else 128), jnp.float32),) * number
        for piece in range(pieces):
            if level == 0:
                @pl.loop(1, nodes)
                def _(k):
                    other = (node + k) % nodes
                    swap(other, piece, other).wait_recv()

            sums = lax.fori_loop(piece * size // 8, (piece + 1) * size // 8, step, sums, unroll=2)
        tile = jnp.zeros(sums_mine.shape[2:], jnp.float32)
        line = lax.broadcasted_iota(jnp.int32, tile.shape, 0)
        for i, term in enumerate(sums):
            tile = jnp.where(line == i, whole_sum(term), tile)
        sums_mine[level, 0] = tile
        sums_mine[level, 1] = exchange(level, 0, count)
        total = exchange(level, 1, nodes)
        return [total[i : i + 1, 0:1] for i in range(number)]

    def coefs(inner, first_sq, second_sq):
        return 1.0 - inner / (2.0 * (first_sq + EPS)), 1.0 - inner / (2.0 * (second_sq + EPS))

    def one_level(level, left):
        def products(part):
            for j in range(left):
                first, second = gathered[j, part, :], gathered[j + left, part, :]
                yield from ((first, second), (first, first), (second, second))

        sums = reduce_all(level, products, 3 * left)
        for j in range(left):
            coef_first, coef_second = coefs(*sums[3 * j : 3 * j + 3])

            def mix(part, carry):
                terms = coef_first * gathered[j, part, :], coef_second * gathered[j + left, part, :]
                if left == 1:
                    out_ref[0, part, :], out_ref[1, part, :] = terms
                else:
                    gathered[j, part, :] = terms[0] + terms[1]

            by_chunk(mix)

    def two_levels(level):
        def products(part):
            bases = []
            for j in range(2):
                first, second = gathered[j, part, :], gathered[j + 2, part, :]
                both = first + second
                bases.append((first, second, both))
                yield from ((first, second), (first, first), (second, second), (both, both), (both, first - second))
            for left in bases[0]:
                for right in bases[1]:
                    yield left, right

        sums = reduce_all(level, products, 19)
        pairs = []
        for j in range(2):
            inner, first_sq, second_sq, both_sq, cross = sums[5 * j : 5 * j + 5]
            first, second = coefs(inner, first_sq, second_sq)
            cancels = both_sq < 0.25 * (first_sq + second_sq)
            mean = 0.5 * (first + second)
            gap = 0.25 * (inner / (first_sq + EPS)) * (cross / (second_sq + EPS))
            plain = first * (first * first_sq) + 2.0 * (first * (second * inner)) + second * (second * second_sq)
            apart_sq = first_sq + second_sq - 2.0 * inner
            by_sum = mean * (mean * both_sq) + 2.0 * (mean * (gap * cross)) + gap * (gap * apart_sq)
            weights = (jnp.where(cancels, gap, first), jnp.where(cancels, -gap, second), mean)
            pairs.append((first, second, jnp.where(cancels, by_sum, plain), cancels, weights))
        inner = jnp.zeros((1, 1), jnp.float32)
        for i in range(3):
            for k in range(3):
                term = pairs[0][4][i] * (pairs[1][4][k] * sums[10 + 3 * i + k])
                if i == 2:
                    term = jnp.where(pairs[0][3], term, 0.0)
                if k == 2:
                    term = jnp.where(pairs[1][3], term, 0.0)
                inner = inner + term
        low, high = coefs(inner, pairs[0][2], pairs[1][2])

        def mix(part, carry):
            below = pairs[0][0] * gathered[0, part, :] + pairs[0][1] * gathered[2, part, :]
            above = pairs[1][0] * gathered[1, part, :] + pairs[1][1] * gathered[3, part, :]
            out_ref[0, part, :] = low * below
            out_ref[1, part, :] = high * above

        by_chunk(mix)

    level, matrices = 0, nodes
    while matrices > 1:
        if matrices == 4:
            two_levels(level)
            break
        matrices //= 2
        one_level(level, matrices)
        level += 1

    @pl.loop(1, nodes)
    def _(k):
        for piece in range(pieces):
            swap((node + k) % nodes, piece, node).wait_send()

    @pl.loop(0, nodes // 2)
    def _(pair):
        for parity in range(2):
            for side in range(2):
                @pl.loop(0, hops(side, parity))
                def _(step):
                    data, top = copies(side, 2 * pair + parity, step)
                    top.wait_send()
                    data.wait_send()


def solution(mesh):
    nodes, count = mesh.shape["node"], mesh.shape["fsdp"]

    def local(activations, grad_out):
        tokens, features = activations.shape
        columns = grad_out.shape[1]
        rows, cols = features // count, columns // nodes
        half = count // 2
        levels = nodes.bit_length() - 1
        if cols % 128:
            grad_out = grad_out.reshape(tokens, nodes, cols).transpose(1, 0, 2)
        lines = max(24, -(-3 * nodes // 2 // 8) * 8)
        hop = (2, nodes, half)
        pieces = 2 if rows % (4 * CHUNK) else 4
        dma = pltpu.SemaphoreType.DMA
        terms = pl.pallas_call(
            functools.partial(kernel, nodes, count),
            out_shape=jax.ShapeDtypeStruct((2, rows, cols), jnp.float32),
            in_specs=[pl.BlockSpec(memory_space=pl.ANY)] * 2,
            out_specs=pl.BlockSpec(memory_space=pltpu.VMEM),
            scratch_shapes=[
                pltpu.VMEM((tokens, features), jnp.bfloat16),
                pltpu.VMEM((features, tokens), jnp.bfloat16),
                pltpu.VMEM(grad_out.shape, jnp.bfloat16),
                pltpu.VMEM(hop + (rows, cols), jnp.bfloat16),
                pltpu.VMEM(hop + (rows, cols), jnp.bfloat16),
                pltpu.VMEM(hop + (16, 128), jnp.bfloat16),
                pltpu.VMEM(hop + (16, 128), jnp.bfloat16),
                pltpu.VMEM((rows, cols), jnp.float32),
                pltpu.VMEM((CHUNK, cols), jnp.float32),
                pltpu.VMEM((nodes, rows, cols), jnp.float32),
                pltpu.VMEM((nodes, rows, cols), jnp.float32),
                pltpu.VMEM((levels, 2, lines, 128), jnp.float32),
                pltpu.VMEM((levels, 2, max(nodes, count), lines, 128), jnp.float32),
                dma((Z_SIZE,)), dma((nodes,)),
                dma(hop), dma(hop), dma(hop), dma(hop),
                dma((nodes, pieces)), dma((nodes, pieces)),
                dma((levels, 2, max(nodes, count))), dma((levels, 2, max(nodes, count))),
            ],
            compiler_params=pltpu.CompilerParams(
                collective_id=0, has_side_effects=True, vmem_limit_bytes=60 * 2**20),
        )(activations, grad_out)
        return terms[0] + terms[1]

    in_specs = (P(("node", "fsdp"), None), P(("node", "fsdp"), None))
    return jax.shard_map(local, mesh=mesh, in_specs=in_specs, out_specs=P("fsdp", "node"), check_vma=False)
```

```python
import functools

import jax
import jax.numpy as jnp
from jax import lax
from jax.experimental import pallas as pl
from jax.experimental.pallas import tpu as pltpu
from jax.sharding import PartitionSpec as P

EPS = 1e-06
MESH = pl.DeviceIdType.MESH
TOP = 2.0**14
Z_SIZE = 4
CHUNK = 16


def ring_place(position, count):
    x_size = count // Z_SIZE
    inner = x_size - 1
    past = (position + count - Z_SIZE) // count
    rest = (position - Z_SIZE + count) % count
    line = rest // inner
    step = rest % inner
    odd = line % 2
    x = (1 - odd) * (1 + step) + odd * (x_size - 1 - step)
    z = Z_SIZE - 1 - line
    return past * (z * x_size + x) + (1 - past) * position * x_size


def ring_position(index, count):
    x_size = count // Z_SIZE
    inner = x_size - 1
    z = index // x_size
    x = index % x_size
    past = (x + inner) // x_size
    line = Z_SIZE - 1 - z
    odd = line % 2
    step = (1 - odd) * (x - 1) + odd * (x_size - 1 - x)
    return past * (Z_SIZE + line * inner + step) + (1 - past) * z


def encode(value, scale):
    x = value * scale
    square = x * x
    fourth = square * square
    eighth = fourth * fourth
    return jnp.where(x < 0, -eighth, eighth).astype(jnp.bfloat16)


def decode(code, top):
    y = code.astype(jnp.float32)
    root = lax.rsqrt(lax.rsqrt(jnp.maximum(jnp.abs(y), 1e-37)))
    value = root * lax.rsqrt(root) * (top * (1.0 / TOP))
    return jnp.where(y < 0, -value, value)


def kernel(
    nodes, count, a_ref, g_hbm, out_ref,
    raw, at_ref, g_ref, sent, came, acc, peaks, own, gathered, sums_mine, sums_came,
    a_sem, g_sem, send_sem, recv_sem, swap_send, swap_recv, sum_send, sum_recv,
):
    node = lax.axis_index("node")
    place = lax.axis_index("fsdp")
    rows, cols = acc.shape
    pieces = swap_send.shape[1]
    size = rows // pieces
    me = ring_position(place, count)
    right = ring_place((me + 1) % count, count)
    left = ring_place((me + count - 1) % count, count)
    half = count // 2

    x_size = count // Z_SIZE
    width = raw.shape[1] // Z_SIZE
    far_group = ring_place((me + half) % count, count) // x_size

    def pair_at(turn):
        return (node // 2 + 1 + turn) % (nodes // 2)

    def g_view(ref, block):
        if ref.ndim == 3:
            return ref.at[block]
        return ref.at[:, pl.ds(pl.multiple_of(block * cols, cols), cols)]

    def a_load(group):
        part = pl.ds(pl.multiple_of(group * width, 128), width)
        return pltpu.make_async_copy(a_ref.at[:, part], raw.at[:, part], a_sem.at[group])

    def g_load(block):
        return pltpu.make_async_copy(g_view(g_hbm, block), g_view(g_ref, block), g_sem.at[block])

    barrier = pltpu.get_barrier_semaphore()
    for k in range(1, count):
        pl.semaphore_signal(barrier, inc=1, device_id=(node, (place + k) % count), device_id_type=MESH)
    for k in range(1, nodes):
        pl.semaphore_signal(barrier, inc=1, device_id=((node + k) % nodes, place), device_id_type=MESH)
    a_load(far_group).start()
    for parity in range(2):
        g_load(2 * pair_at(0) + parity).start()
    for k in range(1, Z_SIZE):
        a_load((far_group + k) % Z_SIZE).start()

    @pl.loop(1, nodes // 2)
    def _(turn):
        for parity in range(2):
            g_load(2 * pair_at(turn) + parity).start()

    def transpose_group(group):
        a_load(group).wait()

        @pl.loop(0, width // 128)
        def _(i):
            part = pl.ds(pl.multiple_of(group * width + i * 128, 128), 128)
            at_ref[part, :] = raw[:, part].T

    transpose_group(far_group)
    pl.semaphore_wait(barrier, count + nodes - 2)

    def product(owner, block):
        mine = at_ref[pl.ds(pl.multiple_of(owner * rows, 16), rows), :]
        acc[...] = jnp.dot(mine, g_view(g_ref, block)[...], preferred_element_type=jnp.float32)

    wide = sent.shape[-1]
    slabs = cols // wide
    tail = pl.ds(slabs * rows, 16)

    def hop_copy(side, block, step):
        return pltpu.make_async_remote_copy(
            src_ref=sent.at[side, block, step], dst_ref=came.at[side, block, step],
            send_sem=send_sem.at[side, block, step], recv_sem=recv_sem.at[side, block, step],
            device_id=(node, right * (1 - side) + left * side), device_id_type=MESH)

    def slab(part, i):
        return pl.ds(pl.multiple_of(part.start + i * rows, CHUNK), CHUNK)

    def received(side, block, step, part, top):
        codes = [came[side, block, step, slab(part, i), :] for i in range(slabs)]
        return decode(jnp.concatenate(codes, axis=1), top)

    def by_chunk(body, start=None, first=0, number=rows):
        def step(i, carry):
            return body(pl.ds(pl.multiple_of(first + i * CHUNK, CHUNK), CHUNK), carry)

        return lax.fori_loop(0, number // CHUNK, step, start, unroll=5)

    def arrived(side, block, step):
        hop_copy(side, block, step).wait_recv()
        return came[side, block, step, tail, :][0:1, 0:1].astype(jnp.float32)

    def hops(side, parity):
        return half if side == parity else count - 1 - half

    def send_on(side, parity, block, step):
        distance = hops(side, parity) - step
        far = (me + distance) % count if side == 0 else (me + count - distance) % count
        product(ring_place(far, count), block)

        @pl.when(step > 0)
        def _():
            top = arrived(side, block, step - 1)

            def add(part, peak):
                value = acc[part, :] + received(side, block, step - 1, part, top)
                acc[part, :] = value
                return jnp.maximum(peak, jnp.abs(value))

            peaks[...] = by_chunk(add, jnp.zeros(peaks.shape, jnp.float32))

        @pl.when(step == 0)
        def _():
            peaks[...] = by_chunk(
                lambda part, peak: jnp.maximum(peak, jnp.abs(acc[part, :])), jnp.zeros(peaks.shape, jnp.float32))

        largest = jnp.maximum(jnp.max(peaks[...], axis=(0, 1), keepdims=True), 1e-30)
        tile = jnp.broadcast_to(largest, (16, wide)).astype(jnp.bfloat16)
        sent[side, block, step, tail, :] = tile
        scale = TOP / tile[0:1, 0:1].astype(jnp.float32)

        def code(part, carry):
            codes = encode(acc[part, :], scale)
            for i in range(slabs):
                sent[side, block, step, slab(part, i), :] = codes[:, i * wide : (i + 1) * wide]

        by_chunk(code)
        hop_copy(side, block, step).start()

    def swap(block, piece, sender):
        part = pl.ds(pl.multiple_of(piece * size, 8), size)
        return pltpu.make_async_remote_copy(
            src_ref=own.at[block, part], dst_ref=gathered.at[sender, part],
            send_sem=swap_send.at[block, piece], recv_sem=swap_recv.at[sender, piece],
            device_id=(block, place), device_id_type=MESH)

    def prepare(parity, block):
        product(place, block)
        top = arrived(1 - parity, block, half - 2)

        def add(part, carry):
            own[block, part, :] = acc[part, :] + received(1 - parity, block, half - 2, part, top)

        by_chunk(add)

    def finish(parity, block):
        top = arrived(parity, block, half - 1)

        def total(part):
            return own[block, part, :] + received(parity, block, half - 1, part, top)

        @pl.when(block != node)
        def _():
            def store(part, carry):
                own[block, part, :] = total(part)

            for piece in range(pieces):
                by_chunk(store, None, piece * size, size)
                swap(block, piece, node).start()

        @pl.when(block == node)
        def _():
            def store(part, carry):
                gathered[block, part, :] = total(part)

            by_chunk(store)

    def finish_pair(turn):
        for parity in range(2):
            prepare(parity, 2 * pair_at(turn) + parity)
        for parity in (1 - node % 2, node % 2):
            finish(parity, 2 * pair_at(turn) + parity)

    @pl.loop(0, nodes // 2)
    def _(turn):
        pair = pair_at(turn)
        for parity in range(2):
            g_load(2 * pair + parity).wait()

        @pl.loop(0, half)
        def _(step):
            for side in range(2):
                send_on(side, side, 2 * pair + side, step)

            @pl.when((turn == 0) & (step == 0))
            def _():
                for k in (1, Z_SIZE - 1):
                    transpose_group((far_group + k) % Z_SIZE)

            @pl.when(step < half - 1)
            def _():
                for side in range(2):
                    send_on(side, 1 - side, 2 * pair + 1 - side, step)

            @pl.when((turn == 0) & (step == 0))
            def _():
                for k in range(2, Z_SIZE - 1):
                    transpose_group((far_group + k) % Z_SIZE)

            @pl.when((step == 0) & (turn > 0))
            def _():
                finish_pair(turn - 1)

    finish_pair(nodes // 2 - 1)

    def exchange(level, stage, members):
        def copy(k):
            far = (node, (place + k) % count) if stage == 0 else ((node + k) % nodes, place)
            return pltpu.make_async_remote_copy(
                src_ref=sums_mine.at[level, stage], dst_ref=sums_came.at[level, stage, k],
                send_sem=sum_send.at[level, stage, k], recv_sem=sum_recv.at[level, stage, k],
                device_id=far, device_id_type=MESH)

        for k in range(1, members):
            copy(k).start()
        total = sums_mine[level, stage]
        for k in range(1, members):
            copy(k).wait_recv()
            total = total + sums_came[level, stage, k]
        for k in range(1, members):
            copy(k).wait_send()
        return total

    def whole_sum(value):
        return jnp.sum(jnp.sum(value, axis=0, keepdims=True), axis=1, keepdims=True)

    def fold(value):
        if cols % 128:
            return value
        return sum(value[:, i : i + 128] for i in range(0, cols, 128))

    def reduce_all(level, pairs_of, number):
        def step(i, sums):
            part = pl.ds(pl.multiple_of(i * 8, 8), 8)
            return tuple(t + fold(a * b) for t, (a, b) in zip(sums, pairs_of(part)))

        sums = (jnp.zeros((8, cols if cols % 128 else 128), jnp.float32),) * number
        for piece in range(pieces):
            if level == 0:
                @pl.loop(1, nodes)
                def _(k):
                    other = (node + k) % nodes
                    swap(other, piece, other).wait_recv()

            sums = lax.fori_loop(piece * size // 8, (piece + 1) * size // 8, step, sums, unroll=2)
        tile = jnp.zeros(sums_mine.shape[2:], jnp.float32)
        line = lax.broadcasted_iota(jnp.int32, tile.shape, 0)
        for i, term in enumerate(sums):
            tile = jnp.where(line == i, whole_sum(term), tile)
        sums_mine[level, 0] = tile
        sums_mine[level, 1] = exchange(level, 0, count)
        total = exchange(level, 1, nodes)
        return [total[i : i + 1, 0:1] for i in range(number)]

    def coefs(inner, first_sq, second_sq):
        return 1.0 - inner / (2.0 * (first_sq + EPS)), 1.0 - inner / (2.0 * (second_sq + EPS))

    def one_level(level, left):
        def products(part):
            for j in range(left):
                first, second = gathered[j, part, :], gathered[j + left, part, :]
                yield from ((first, second), (first, first), (second, second))

        sums = reduce_all(level, products, 3 * left)
        for j in range(left):
            coef_first, coef_second = coefs(*sums[3 * j : 3 * j + 3])

            def mix(part, carry):
                terms = coef_first * gathered[j, part, :], coef_second * gathered[j + left, part, :]
                if left == 1:
                    out_ref[0, part, :], out_ref[1, part, :] = terms
                else:
                    gathered[j, part, :] = terms[0] + terms[1]

            by_chunk(mix)

    def two_levels(level):
        def products(part):
            bases = []
            for j in range(2):
                first, second = gathered[j, part, :], gathered[j + 2, part, :]
                both = first + second
                bases.append((first, second, both))
                yield from ((first, second), (first, first), (second, second), (both, both), (both, first - second))
            for left in bases[0]:
                for right in bases[1]:
                    yield left, right

        sums = reduce_all(level, products, 19)
        pairs = []
        for j in range(2):
            inner, first_sq, second_sq, both_sq, cross = sums[5 * j : 5 * j + 5]
            first, second = coefs(inner, first_sq, second_sq)
            cancels = both_sq < 0.25 * (first_sq + second_sq)
            mean = 0.5 * (first + second)
            gap = 0.25 * (inner / (first_sq + EPS)) * (cross / (second_sq + EPS))
            plain = first * (first * first_sq) + 2.0 * (first * (second * inner)) + second * (second * second_sq)
            apart_sq = first_sq + second_sq - 2.0 * inner
            by_sum = mean * (mean * both_sq) + 2.0 * (mean * (gap * cross)) + gap * (gap * apart_sq)
            weights = (jnp.where(cancels, gap, first), jnp.where(cancels, -gap, second), mean)
            pairs.append((first, second, jnp.where(cancels, by_sum, plain), cancels, weights))
        inner = jnp.zeros((1, 1), jnp.float32)
        for i in range(3):
            for k in range(3):
                term = pairs[0][4][i] * (pairs[1][4][k] * sums[10 + 3 * i + k])
                if i == 2:
                    term = jnp.where(pairs[0][3], term, 0.0)
                if k == 2:
                    term = jnp.where(pairs[1][3], term, 0.0)
                inner = inner + term
        low, high = coefs(inner, pairs[0][2], pairs[1][2])

        def mix(part, carry):
            below = pairs[0][0] * gathered[0, part, :] + pairs[0][1] * gathered[2, part, :]
            above = pairs[1][0] * gathered[1, part, :] + pairs[1][1] * gathered[3, part, :]
            out_ref[0, part, :] = low * below
            out_ref[1, part, :] = high * above

        by_chunk(mix)

    level, matrices = 0, nodes
    while matrices > 1:
        if matrices == 4:
            two_levels(level)
            break
        matrices //= 2
        one_level(level, matrices)
        level += 1

    @pl.loop(1, nodes)
    def _(k):
        for piece in range(pieces):
            swap((node + k) % nodes, piece, node).wait_send()

    @pl.loop(0, nodes // 2)
    def _(pair):
        for parity in range(2):
            for side in range(2):
                @pl.loop(0, hops(side, parity))
                def _(step):
                    hop_copy(side, 2 * pair + parity, step).wait_send()


def solution(mesh):
    nodes, count = mesh.shape["node"], mesh.shape["fsdp"]

    def local(activations, grad_out):
        tokens, features = activations.shape
        columns = grad_out.shape[1]
        rows, cols = features // count, columns // nodes
        half = count // 2
        levels = nodes.bit_length() - 1
        if cols % 128:
            grad_out = grad_out.reshape(tokens, nodes, cols).transpose(1, 0, 2)
        lines = max(24, -(-3 * nodes // 2 // 8) * 8)
        hop = (2, nodes, half)
        wide = cols if cols % 128 else 128
        pieces = 2 if rows % (4 * CHUNK) else 4
        dma = pltpu.SemaphoreType.DMA
        terms = pl.pallas_call(
            functools.partial(kernel, nodes, count),
            out_shape=jax.ShapeDtypeStruct((2, rows, cols), jnp.float32),
            in_specs=[pl.BlockSpec(memory_space=pl.ANY)] * 2,
            out_specs=pl.BlockSpec(memory_space=pltpu.VMEM),
            scratch_shapes=[
                pltpu.VMEM((tokens, features), jnp.bfloat16),
                pltpu.VMEM((features, tokens), jnp.bfloat16),
                pltpu.VMEM(grad_out.shape, jnp.bfloat16),
                pltpu.VMEM(hop + (cols // wide * rows + 16, wide), jnp.bfloat16),
                pltpu.VMEM(hop + (cols // wide * rows + 16, wide), jnp.bfloat16),
                pltpu.VMEM((rows, cols), jnp.float32),
                pltpu.VMEM((CHUNK, cols), jnp.float32),
                pltpu.VMEM((nodes, rows, cols), jnp.float32),
                pltpu.VMEM((nodes, rows, cols), jnp.float32),
                pltpu.VMEM((levels, 2, lines, 128), jnp.float32),
                pltpu.VMEM((levels, 2, max(nodes, count), lines, 128), jnp.float32),
                dma((Z_SIZE,)), dma((nodes,)),
                dma(hop), dma(hop),
                dma((nodes, pieces)), dma((nodes, pieces)),
                dma((levels, 2, max(nodes, count))), dma((levels, 2, max(nodes, count))),
            ],
            compiler_params=pltpu.CompilerParams(
                collective_id=0, has_side_effects=True, vmem_limit_bytes=60 * 2**20),
        )(activations, grad_out)
        return terms[0] + terms[1]

    in_specs = (P(("node", "fsdp"), None), P(("node", "fsdp"), None))
    return jax.shard_map(local, mesh=mesh, in_specs=in_specs, out_specs=P("fsdp", "node"), check_vma=False)
```
